32 devices in a mesh: gx: 4 (over z), gy: 8 (over y, x, core).
Axes of the slice: x: 2, y: 2, z: 4, core: 2. Of those that a mesh axis runs over, the one named last changes fastest.
Arguments:
- dynamics: float32 [3, 93, 8, 1024], P(None, None, 'gx', 'gy'), may hold values from -4 to 4
- tracers: float32 [33, 93, 8, 1024], P(None, None, 'gx', 'gy'), may hold values from 0.05 to 16
- thickness: float32 [93, 8, 1024], P(None, 'gx', 'gy'), may hold values from 0.005376344 to 0.017204301
- area_weight: float32 [8, 1024], P('gx', 'gy'), may hold values from 0.3 to 3
- cloud_frac: float32 [93, 8192], P(None, ('gx', 'gy')), may hold values from 0.05 to 1
- owner: int32 [8, 1024], P('gx', 'gy'), may hold values from 0 to 31, as said below
- warm_mask: int32 [8, 1024], P('gx', 'gy'), may hold values 0 or 1
Outputs:
- dynamics_new: float32 [3, 93, 8, 1024], P(None, None, 'gx', 'gy')
- tracers_new: float32 [33, 93, 8, 1024], P(None, None, 'gx', 'gy')
- increment_stack: float32 [4, 93, 8, 1024], P(None, None, 'gx', 'gy')
- cloud_next: float32 [93, 8192], P(None, ('gx', 'gy'))
The draws below stay inside these ranges and needn't reach their ends.
Inputs may be any that keep to these rules, and one draw needn't show every extreme that they name: Every device along gx+gy owns exactly 256 columns; the columns of one device that go to one owner number at most 16.
All inputs are finite; a program needn't handle non-finite values. No bound on the sum of `warm_mask` on one device may be relied on, other than what follows from the above.
Results may differ from the reference program's by a relative error of at most 0.0003.
Values sent between devices are 32-bit elements; how exact they have to be, the bound alone decides.
No kernel may reach another device: no remote copies, remote signals or barrier semaphores. Data moves between devices by JAX's collectives and lax.ppermute only.
A program may use at most 128 MiB of HBM per device.

```python
import math
import jax
import jax.numpy as jnp
from jax import lax

L = 93
Q = 33
NDYN = 3
NP = 4
AX = 2
BY = 128
NX = 8
NY = 1024
NCOLS = 8192
N_GX = 4
N_GY = 8


def draw_owner(key, part):
    devices = N_GX * N_GY
    per_device = AX * BY
    capacity = 2 * per_device // devices
    key_half, key_offset, key_shift, key_order = jax.random.split(key, 4)
    halves = jax.random.randint(key_half, (devices // 2,), 0, capacity + 1)
    halves = halves.at[0].set(capacity)
    counts = jnp.stack([halves, capacity - halves], axis=1).reshape(devices)
    offsets = jax.random.permutation(key_offset, devices)
    shifts = jax.random.permutation(key_shift, devices)
    bounds = jnp.cumsum(counts)
    orders = jax.vmap(lambda single: jax.random.permutation(single, per_device))(jax.random.split(key_order, devices))
    which = jnp.sum((bounds[None, None, :] <= orders[:, :, None]).astype(jnp.int32), axis=2)
    dest = (shifts[:, None] + offsets[which]) % devices
    grid = jnp.transpose(dest.reshape(N_GX, N_GY, AX, BY), (0, 2, 1, 3)).reshape(N_GX * AX, N_GY * BY)
    return grid.astype(jnp.int32)


def draw_thickness(key, part):
    lower = 0.5 / L
    upper = 1.6 / L
    key_sign, key_strength, key_noise = jax.random.split(jax.random.fold_in(key, 7), 3)
    groups = NY // 32
    signs = 2.0 * jax.random.randint(key_sign, (groups,), 0, 2).astype(jnp.float32) - 1.0
    strength = jax.random.uniform(key_strength, (groups,), jnp.float32, 0.3, 0.4)
    noise = jax.random.uniform(key_noise, (L, NX, NY), jnp.float32, -0.1, 0.1)
    profile = jnp.repeat(signs * strength, 32)
    height = jnp.arange(L).astype(jnp.float32) / (L - 1)
    level_trend = 1.0 - 2.0 * height
    share = 0.5 + profile[None, None, :] * level_trend[:, None, None] + noise
    share = jnp.clip(share, 0.0, 1.0)
    return (lower * jnp.exp(jnp.log(upper / lower) * share)).astype(jnp.float32)


def plant(entries, stream_key, smallest, largest):
    longest = entries.shape.index(max(entries.shape))
    spots = []
    for shift in (0, 1):
        where = [jax.random.randint(jax.random.fold_in(stream_key, axis), (), 0, length) for axis, length in enumerate(entries.shape)]
        where[longest] = (where[longest] + shift) % entries.shape[longest]
        spots.append(tuple(where))
    return entries.at[spots[0]].set(smallest).at[spots[1]].set(largest)


def levels(stream_key, shape, cuts, least, top_value):
    factor_of = 1.0
    for dim, parts in cuts:
        heights = jax.random.uniform(jax.random.fold_in(jax.random.fold_in(stream_key, 6), dim), (parts,), jnp.float32, least / len(cuts), top_value / len(cuts))
        factor_of = factor_of * jnp.repeat(jnp.exp(heights), shape[dim] // parts).reshape((-1,) + (1,) * (len(shape) - 1 - dim))
    return factor_of


def bell_draw(rng, extent, spread, most, cuts=(), kind=jnp.bfloat16):
    values = spread * jax.random.normal(rng, extent, jnp.float32)
    if cuts:
        values = values * levels(rng, extent, cuts, -0.22, 0.18)
    return jnp.clip(values, -most, most).astype(kind)


def setup_inputs(seed: int = 0) -> dict:
    key_of = jax.random.split(jax.random.key(seed), 8)
    dynamics = bell_draw(key_of[0], (NDYN, L, NX, NY), 1.0, 4.0, ((2, 4), (3, 8)), jnp.float32)
    tracers = jnp.clip(jnp.exp(math.log(16.0) - 5.768321 * jax.random.uniform(key_of[1], (Q, L, NX, NY), jnp.float32) ** levels(key_of[1], (Q, L, NX, NY), ((2, 4), (3, 8)), -0.2, 0.2)), 0.05, 16.0)
    thickness = draw_thickness(jax.random.fold_in(key_of[7], 71), 0)
    area_weight = jnp.clip(jnp.exp(math.log(3.0) - 2.3025851 * jax.random.uniform(key_of[3], (NX, NY), jnp.float32) ** levels(key_of[3], (NX, NY), ((0, 4), (1, 8)), -0.2, 0.2)), 0.3, 3.0)
    cloud_frac = jnp.clip(jnp.exp(math.log(1.0) - 2.9957323 * jax.random.uniform(key_of[4], (L, NCOLS), jnp.float32) ** levels(key_of[4], (L, NCOLS), ((1, 32),), -0.2, 0.2)), 0.05, 1.0)
    owner = draw_owner(jax.random.fold_in(key_of[7], 71), 0)
    warm_mask = plant((jax.random.randint(key_of[6], (NX, NY), 0, 5) < 2).astype(jnp.int32), jax.random.fold_in(key_of[6], 1), 0, 1)
    return {"dynamics": dynamics, "tracers": tracers, "thickness": thickness, "area_weight": area_weight, "cloud_frac": cloud_frac, "owner": owner, "warm_mask": warm_mask}


top_pressure = 0.002
mid_pressure = 0.6
kappa_sat = 0.06
phase_change_warming = 0.25
auto_rate = 0.8
accrete_rate = 0.5
fall_rate = 20.0


def target_edges(ground_deposit_rate, number_of_layers_total):
    sigma = (jnp.arange(number_of_layers_total + 1).astype(ground_deposit_rate.dtype) / number_of_layers_total)[:, None]
    return top_pressure * (1.0 - sigma) + sigma * sigma * ground_deposit_rate[None, :] + sigma * (1.0 - sigma) * mid_pressure


def remap_block(fields, thick):
    number_of_layers_total = thick.shape[0]
    source = jnp.concatenate([jnp.full((1, thick.shape[1]), top_pressure, thick.dtype), top_pressure + jnp.cumsum(thick, axis=0)], 0)
    ground_deposit_rate = source[-1]
    target = target_edges(ground_deposit_rate, number_of_layers_total)
    thick_tgt = target[1:] - target[:-1]
    frac = jnp.clip((target[:, None, :] - source[None, :-1, :]) / thick[None], 0.0, 1.0)
    powers = jnp.stack([frac, frac * frac * 0.5, frac * frac * frac / 3.0])
    below = jnp.concatenate([fields[:, :1], fields[:, :-1]], 1)
    above = jnp.concatenate([fields[:, 1:], fields[:, -1:]], 1)
    above_two = jnp.concatenate([fields[:, 2:], fields[:, -1:], fields[:, -1:]], 1)
    edge = (7.0 / 12.0) * (fields + above) - (1.0 / 12.0) * (below + above_two)
    edge = jnp.clip(edge, jnp.minimum(fields, above), jnp.maximum(fields, above))
    left = jnp.concatenate([fields[:, :1], edge[:, :-1]], 1)
    sixth = 6.0 * fields - 3.0 * (left + edge)
    coeffs = jnp.stack([left, edge - left + sixth, -sixth]) * thick[None, None]
    cumulative = jnp.einsum("jtkc,jfkc->ftc", powers, coeffs, precision=lax.Precision.HIGHEST)
    return (cumulative[:, 1:] - cumulative[:, :-1]) / thick_tgt[None], ground_deposit_rate


def vertical_profile_microscale(ambient_kelvin_state, moisture_mixratio, droplet_mixratio, falling_drops_mixratio, ground_deposit_rate, present_droplet_mixratio, above_freezing_marker):
    number_of_layers_total = ambient_kelvin_state.shape[0]
    edges = target_edges(ground_deposit_rate, number_of_layers_total)
    layer = edges[1:] - edges[:-1]
    middle = 0.5 * (edges[1:] + edges[:-1])
    centigrade_reading = 10.0 * ambient_kelvin_state
    saturation = 3.8 / middle * jnp.exp(17.27 * centigrade_reading / (centigrade_reading + 237.3))
    phase_change_mass = jnp.maximum((moisture_mixratio - saturation) / (1.0 + kappa_sat * saturation), -droplet_mixratio)
    revised_moisture_mixratio = moisture_mixratio - phase_change_mass
    liquid_mid = droplet_mixratio + phase_change_mass
    revised_kelvin_state = ambient_kelvin_state + phase_change_warming * phase_change_mass
    converted = liquid_mid * (1.0 - jnp.exp(-(auto_rate * present_droplet_mixratio + accrete_rate * falling_drops_mixratio)))
    warm = (above_freezing_marker == 1)[None, :]
    revised_droplet_mixratio = jnp.where(warm, liquid_mid - converted, liquid_mid)
    rain_mid = jnp.where(warm, falling_drops_mixratio + converted, falling_drops_mixratio)
    falling = fall_rate * (0.5 + present_droplet_mixratio)

    def descend(outflow, inputs):
        amount, speed = inputs
        kept = (amount + outflow) / (1.0 + speed)
        return speed * kept, kept

    outflow_end, settled = lax.scan(descend, jnp.zeros_like(ground_deposit_rate), (rain_mid * layer, falling))
    revised_drops_mixratio = jnp.where(warm, settled / layer, rain_mid)
    target = jnp.clip((revised_moisture_mixratio / saturation - 0.7) / 0.3, 0.05, 1.0)
    cloud_new = present_droplet_mixratio + 0.5 * (target - present_droplet_mixratio)
    increment_stack = jnp.stack([revised_kelvin_state - ambient_kelvin_state, revised_moisture_mixratio - moisture_mixratio, revised_droplet_mixratio - droplet_mixratio, revised_drops_mixratio - falling_drops_mixratio])
    return increment_stack, cloud_new


def edge_sum(field):
    rows = jnp.arange(NX) % AX
    first = (rows == 0)[:, None]
    last = (rows == AX - 1)[:, None]
    summed = field + jnp.where(first, jnp.roll(field, 1, axis=-2), 0.0) + jnp.where(last, jnp.roll(field, -1, axis=-2), 0.0)
    cols = jnp.arange(NY) % NP
    first_col = cols == 0
    last_col = cols == NP - 1
    return summed + jnp.where(first_col, jnp.roll(summed, 1, axis=-1), 0.0) + jnp.where(last_col, jnp.roll(summed, -1, axis=-1), 0.0)


def to_cols(array):
    lead = array.shape[:-2]
    shaped = array.reshape(lead + (N_GX, AX, N_GY, BY))
    return jnp.swapaxes(shaped, -3, -2).reshape(lead + (NCOLS,))


def from_cols(array):
    lead = array.shape[:-1]
    shaped = array.reshape(lead + (N_GX, N_GY, AX, BY))
    return jnp.swapaxes(shaped, -3, -2).reshape(lead + (NX, NY))


def reference(dynamics, tracers, thickness, area_weight, cloud_frac, owner, warm_mask):
    weight = area_weight[None] * thickness
    mass = edge_sum(weight)
    area = edge_sum(area_weight)
    thick_new = mass / area[None]
    dyn_new = lax.map(lambda field: edge_sum(weight * field), dynamics) / mass[None]
    trc_new = lax.map(lambda field: edge_sum(weight * field), tracers) / mass[None]
    fields = jnp.concatenate([to_cols(dyn_new), to_cols(trc_new)], 0)
    thick_cols = to_cols(thick_new)
    count = fields.shape[0]
    blocks = NCOLS // 128
    field_blocks = jnp.transpose(fields.reshape(count, L, blocks, 128), (2, 0, 1, 3))
    thick_blocks = jnp.transpose(thick_cols.reshape(L, blocks, 128), (1, 0, 2))
    remapped, ground_deposit_rate = lax.map(lambda pair: remap_block(pair[0], pair[1]), (field_blocks, thick_blocks))
    remapped = jnp.transpose(remapped, (1, 2, 0, 3)).reshape(count, L, NCOLS)
    ground_deposit_rate = ground_deposit_rate.reshape(NCOLS)
    order = jnp.argsort(to_cols(owner), stable=True)
    cloud_cols = jnp.zeros((L, NCOLS), cloud_frac.dtype).at[:, order].set(cloud_frac)
    increment_stack, cloud_new = vertical_profile_microscale(remapped[0], remapped[NDYN], remapped[NDYN + 1], remapped[NDYN + 2], ground_deposit_rate, cloud_cols, to_cols(warm_mask))
    return (from_cols(remapped[:NDYN]), from_cols(remapped[NDYN:]), from_cols(increment_stack), cloud_new[:, order])
```

```python
import numpy as np
import jax
import jax.numpy as jnp
from jax import lax
from jax.experimental import pallas as pl
from jax.experimental.pallas import tpu as pltpu
from jax.sharding import PartitionSpec as P

NP = 4
top_pressure = 0.002
mid_pressure = 0.6
kappa_sat = 0.06
phase_change_warming = 0.25
auto_rate = 0.8
accrete_rate = 0.5
fall_rate = 20.0
THICK_MIN = 0.005376344
THICK_MAX = 0.017204301

LANES = 128
HALF = LANES // 2
PART = LANES // NP
TYPES = NP - 1
PARAMS = 6
VM = pl.BlockSpec(memory_space=pltpu.VMEM)
ANY = pl.BlockSpec(memory_space=pl.ANY)
F32 = jnp.float32
BF16 = jnp.bfloat16


def params(vmem=48):
    return pltpu.CompilerParams(vmem_limit_bytes=vmem * 1024 * 1024)


def cost(us):
    return pl.CostEstimate(flops=0, bytes_accessed=int(us * 3.0e6), transcendentals=0)


def source_windows(levels):
    slack = 1e-4
    lo, hi = THICK_MIN * (1 - slack), THICK_MAX * (1 + slack)
    k = np.arange(levels)
    surfaces = np.linspace(top_pressure + levels * lo, top_pressure + levels * hi, 4001)[:, None]
    least = np.maximum(top_pressure + lo * k, surfaces - hi * (levels - k))
    most = np.minimum(top_pressure + hi * k, surfaces - lo * (levels - k))
    out = []
    for t in range(1, levels + 1):
        s = t / levels
        p = top_pressure * (1 - s) + s * s * surfaces + s * (1 - s) * mid_pressure
        first = np.min(np.sum(most <= p, axis=1)) - 1
        last = np.max(np.sum(least <= p, axis=1)) - 1
        out.append((max(int(first) - 1, 0), min(int(last) + 1, levels - 1)))
    return out


def tile_windows(levels):
    per_edge = source_windows(levels)
    tiles = -(-levels // 8)
    out = []
    for j in range(tiles):
        rows = per_edge[8 * j : min(8 * j + 8, levels)]
        out.append((min(r[0] for r in rows), max(r[1] for r in rows)))
    return out


def pack_matrix():
    m = np.zeros((NP * LANES, TYPES * LANES), np.float32)
    for b in range(NP):
        for e in range(PART):
            m[b * LANES + NP * e, b * PART + e] = 1
            if e:
                m[b * LANES + NP * e - 1, b * PART + e] = 1
            m[b * LANES + NP * e + 1, LANES + b * PART + e] = 1
            m[b * LANES + NP * e + 2, 2 * LANES + b * PART + e] = 1
    return m


def weight_matrix():
    m = np.zeros((LANES, LANES), np.float32)
    for e in range(PART):
        for base in (0, 3 * PART):
            m[NP * e, base + e] = 1
            if e:
                m[NP * e - 1, base + e] = 1
        m[NP * e + 1, PART + e] = 1
        m[NP * e + 2, 2 * PART + e] = 1
    return m


def split2(x):
    top = x.astype(BF16)
    return top, (x - top.astype(F32)).astype(BF16)


def dot(a, b):
    return jnp.dot(a, b, preferred_element_type=F32)


def select_dot2(x, m):
    rows = x.shape[0]
    top, low = split2(x)
    return dot(top, m) + dot(low, m)


def select_dot3(x, m):
    top = x.astype(BF16)
    rest = x - top.astype(F32)
    mid = rest.astype(BF16)
    low = (rest - mid.astype(F32)).astype(BF16)
    return dot(top, m) + dot(mid, m) + dot(low, m)


def lane_iota(rows):
    return lax.broadcasted_iota(jnp.int32, (rows, LANES), 1)


def row_iota(rows):
    return lax.broadcasted_iota(jnp.int32, (rows, LANES), 0)


def pick_lanes(x, index):
    return jnp.take_along_axis(x, index, axis=1, mode="promise_in_bounds")


def prefix_rows(x):
    tiles = x.shape[0] // 8
    row = row_iota(8)
    carry = jnp.zeros((8, LANES), F32)
    out = []
    for j in range(tiles):
        part = x[8 * j : 8 * j + 8]
        for step in (1, 2, 4):
            part = part + jnp.where(row >= step, pltpu.roll(part, step, 0), 0.0)
        part = part + carry
        carry = jnp.broadcast_to(part[7:8], (8, LANES))
        out.append(part)
    return jnp.concatenate(out, 0)


def field_rows(dyn, trc, levels, which, x):
    source, index = which
    ref = dyn if source == 0 else trc
    return ref[pl.ds(index * 2 * levels + x, levels, stride=2), :]


def pack_quad(dyn, trc, weight, m, quad, x, levels):
    rows = jnp.concatenate(
        [weight[x] * field_rows(dyn, trc, levels, which, x) for which in quad], 1
    )
    return select_dot2(rows, m)


def flat(ref):
    lead = 1
    for size in ref.shape[:-1]:
        lead *= size
    return ref.reshape(lead, LANES)


def first_kernel(levels, quad, ndyn, ntrc, dyn4, trc4, thick3, area_ref, m_ref, mw_ref, up_ref, down_ref, edge_ref):
    dyn, trc, thick = flat(dyn4), flat(trc4), flat(thick3)
    weight = [area_ref[x : x + 1, :] * thick[pl.ds(x, levels, stride=2), :] for x in range(2)]
    m = m_ref[...]
    for x, out in ((0, down_ref), (1, up_ref)):
        packed = pack_quad(dyn, trc, weight, m, quad, x, levels)
        for kind in range(TYPES):
            out[kind, 0:levels, :] = packed[:, kind * LANES : (kind + 1) * LANES]
        out[TYPES, 0:levels, :] = select_dot3(weight[x], mw_ref[...])
        area = jnp.broadcast_to(area_ref[x : x + 1, :], (8, LANES))
        out[TYPES, levels : levels + 1, :] = select_dot3(area, mw_ref[...])[0:1]
    lane = lane_iota(levels)
    ends = jnp.where(lane < HALF, 0, LANES - 1)
    spot = lane % HALF
    fields = [(0, i) for i in range(ndyn)] + [(1, i) for i in range(ntrc)]
    for x in range(2):
        total = jnp.zeros((levels, LANES), F32)
        for number, which in enumerate(fields):
            here = pick_lanes(field_rows(dyn, trc, levels, which, x), ends)
            total = jnp.where(spot == number, here, total)
        both = pick_lanes(weight[x], ends)
        total = jnp.where(spot == len(fields), 1.0, total) * both
        edge_ref[x, 0:levels, :] = total
        edge_ref[x, levels : levels + 1, :] = pick_lanes(
            jnp.broadcast_to(area_ref[x : x + 1, :], (8, LANES)), ends[0:8]
        )[0:1]


def pack_kernel(levels, chunks, dyn4, trc4, thick3, area_ref, m_ref, *outs):
    dyn, trc, thick = flat(dyn4), flat(trc4), flat(thick3)
    weight = [area_ref[x : x + 1, :] * thick[pl.ds(x, levels, stride=2), :] for x in range(2)]
    m = m_ref[...]
    for number, quads in enumerate(chunks):
        up_ref, down_ref = outs[2 * number], outs[2 * number + 1]
        for i, quad in enumerate(quads):
            for x, out in ((0, down_ref), (1, up_ref)):
                packed = pack_quad(dyn, trc, weight, m, quad, x, levels)
                for kind in range(TYPES):
                    out[TYPES * i + kind, 0:levels, :] = packed[:, kind * LANES : (kind + 1) * LANES]


def edge_kernel(own_ref, before_ref, after_ref, row0_ref, row1_ref):
    left = lane_iota(own_ref.shape[1]) < HALF
    for x, out in ((0, row0_ref), (1, row1_ref)):
        out[...] = own_ref[x] + jnp.where(
            left, pltpu.roll(before_ref[x], HALF, 1), pltpu.roll(after_ref[x], HALF, 1)
        )


def remap_group(levels, windows, summed, rm, thick, al, ar, aq, rdt, tile_of, row_of, s_ref):
    rows = summed.shape[0]
    tiles = rows // 8
    q = summed * rm
    first = q[0:1]
    last = jnp.broadcast_to(q[levels - 1 : levels], (rows - levels + 2, LANES))
    s_ref[0, 8 : 8 + rows, :] = q
    s_ref[0, 7:8, :] = first
    s_ref[0, 8 + levels : 10 + rows, :] = last
    below = s_ref[0, 7 : 7 + rows, :]
    q = s_ref[0, 8 : 8 + rows, :]
    above = s_ref[0, 9 : 9 + rows, :]
    above_two = s_ref[0, 10 : 10 + rows, :]
    edge = 7.0 / 12.0 * (q + above) - 1.0 / 12.0 * (below + above_two)
    edge = jnp.clip(edge, jnp.minimum(q, above), jnp.maximum(q, above))
    s_ref[1, 8 : 8 + rows, :] = edge
    s_ref[1, 7:8, :] = first
    left = s_ref[1, 7 : 7 + rows, :]
    layer = thick * q
    through = prefix_rows(layer) - layer
    for j in range(tiles):
        low, high = windows[j][0] // 8, windows[j][1] // 8
        part = slice(8 * j, 8 * j + 8)
        tile, row = tile_of[part], row_of[part]
        got = None
        for v in range(low, high + 1):
            here = [
                jnp.take_along_axis(a[8 * v : 8 * v + 8], row, axis=0, mode="promise_in_bounds")
                for a in (through, left, edge, q)
            ]
            if got is None:
                got = here
            else:
                got = [jnp.where(tile == v, new, old) for new, old in zip(here, got)]
        s_ref[2, 8 + 8 * j : 16 + 8 * j, :] = (
            got[0] + al[part] * got[1] + ar[part] * got[2] + aq[part] * got[3]
        )
    s_ref[2, 7:8, :] = jnp.zeros((1, LANES), F32)
    return (s_ref[2, 8 : 8 + rows, :] - s_ref[2, 7 : 7 + rows, :]) * rdt


def column_surface(weights_surface, edge_surface):
    lane = lane_iota(8)
    spot, kind = lane // NP, lane % NP
    index = jnp.where(kind == 3, jnp.minimum(spot + 1, PART - 1), kind * PART + spot)
    inner = pick_lanes(weights_surface, index)
    return jnp.where((lane == 0) | (lane == LANES - 1), edge_surface, inner)


def setup_kernel(levels, nfields, own0, own1, from_up, from_down, row0, row1, edge_up, edge_down, p_ref, i_ref, e_ref, surface_ref, s_ref):
    windows = tile_windows(levels)
    rows = row0.shape[0]
    tiles = rows // 8
    row = row_iota(rows)
    lane = lane_iota(rows)
    inside = row < levels
    edge_lanes = jnp.where(lane < HALF, nfields, HALF + nfields)
    kept = []
    for base in range(4):
        x = base % 2
        own, got = ((own0, from_up), (own1, from_down))[x]
        eown, egot = ((row0, edge_up), (row1, edge_down))[x]
        if base < 2:
            mass = own[TYPES] + got[TYPES]
        else:
            summed = eown[...] + egot[...]
            mass = pick_lanes(summed, edge_lanes)
        area = mass[levels : levels + 1]
        mass = jnp.where(inside, mass, 1.0)
        thick = jnp.where(inside, mass / area, 1.0)
        after = top_pressure + prefix_rows(thick)
        surface = after[levels - 1 : levels]
        s_ref[0, 8 : 8 + rows, :] = after
        s_ref[0, 7:8, :] = jnp.full((1, LANES), top_pressure, F32)
        s_ref[1, 0:rows, :] = thick
        sigma = (row + 1).astype(F32) / levels
        sigma0 = row.astype(F32) / levels

        def target_at(s):
            return top_pressure * (1.0 - s) + s * s * surface + s * (1.0 - s) * mid_pressure

        target = target_at(sigma)
        rdt = jnp.where(inside, 1.0 / (target - target_at(sigma0)), 1.0)
        index, start, depth = [], [], []
        for j in range(tiles):
            low, high = windows[j]
            here = target[8 * j : 8 * j + 8]
            count = jnp.full((8, LANES), low, jnp.int32)
            source = jnp.broadcast_to(s_ref[0, 7 + low : 8 + low, :], (8, LANES))
            size = jnp.broadcast_to(s_ref[1, low : low + 1, :], (8, LANES))
            for k in range(low + 1, high + 1):
                edge_k = jnp.broadcast_to(s_ref[0, 7 + k : 8 + k, :], (8, LANES))
                size_k = jnp.broadcast_to(s_ref[1, k : k + 1, :], (8, LANES))
                reached = edge_k <= here
                count = jnp.where(reached, k, count)
                source = jnp.where(reached, edge_k, source)
                size = jnp.where(reached, size_k, size)
            index.append(count)
            start.append(source)
            depth.append(size)
        index, start, depth = (jnp.concatenate(a, 0) for a in (index, start, depth))
        f = jnp.clip((target - start) / depth, 0.0, 1.0)
        f2, f3 = f * f, f * f * f
        values = [
            1.0 / mass,
            thick,
            depth * (f - 2.0 * f2 + f3),
            depth * (f3 - f2),
            depth * (3.0 * f2 - 2.0 * f3),
            rdt,
        ]
        tile_of, row_of = index >> 3, index & 7
        if base < 2:
            for kind in range(TYPES):
                lanes = kind * PART + lane % PART
                group = 2 * kind + x
                for i, value in enumerate(values):
                    p_ref[group, i] = pick_lanes(value, lanes)
                i_ref[group, 0] = pick_lanes(tile_of, lanes)
                i_ref[group, 1] = pick_lanes(row_of, lanes)
            kept.append(jnp.broadcast_to(surface, (8, LANES)))
        else:
            e_ref[x] = remap_group(levels, windows, summed, *values, tile_of, row_of, s_ref)
            surface_ref[0:1, x * LANES : (x + 1) * LANES] = column_surface(
                kept[x], jnp.broadcast_to(surface, (8, LANES))
            )[0:1]


def remap_kernel(levels, quads, aliased, own0, own1, from_up, from_down, p_ref, i_ref, e_ref, mt_ref, *rest):
    if aliased:
        rest = rest[2:]
        dyn_ref, trc_ref = rest[:2]
        columns_ref = None
        rest = rest[2:]
    else:
        dyn_ref, trc_ref, columns_ref = rest[:3]
        rest = rest[3:]
    s_ref, packed_ref, out_ref, sems = rest
    windows = tile_windows(levels)
    rows = e_ref.shape[1]
    lane = lane_iota(levels)
    ends = (lane == 0) | (lane == LANES - 1)
    half = jnp.where(lane < HALF, 0, HALF)
    out_rows = flat(out_ref)
    fields = TYPES + 1

    ndyn = sum(1 for which in sum(quads, []) if which[0] == 0)

    def numbers(i, b):
        source, index = quads[0][b]
        first = index + (0 if source == 0 else 3)
        return first

    def one_quad(i, edge_lane):
        for kind in range(TYPES):
            for x in range(2):
                group = 2 * kind + x
                own, got = ((own0, from_up), (own1, from_down))[x]
                summed = own[TYPES * i + kind] + got[TYPES * i + kind]
                values = [p_ref[group, n] for n in range(PARAMS)]
                packed_ref[x * rows : (x + 1) * rows, kind * LANES : (kind + 1) * LANES] = remap_group(
                    levels, windows, summed, *values, i_ref[group, 0], i_ref[group, 1], s_ref.at[x]
                )
        wide = select_dot2(packed_ref[...], mt_ref[...])
        for b in range(fields):
            for x in range(2):
                value = wide[x * rows : x * rows + levels, b * LANES : (b + 1) * LANES]
                outer = pick_lanes(e_ref[x, 0:levels, :], half + edge_lane(b))
                value = jnp.where(ends, outer, value)
                out_rows[pl.ds((i * fields + b) * 2 * levels + x, levels, stride=2), :] = value
                if columns_ref is not None:
                    columns_ref[b, 0:levels, x * LANES : (x + 1) * LANES] = value

    table = [[index + (0 if source == 0 else 3) for source, index in quad] for quad in quads]
    copies = []
    for i, quad in enumerate(quads):
        if i == 0 or len(quads) == 1:
            pass
    if len(quads) == 1:
        one_quad(0, lambda b: table[0][b])
    else:
        steps = [table[i][b] - 4 * i for i in range(len(quads)) for b in range(fields)]
        base = table[0]
        regular = all(table[i][b] == base[b] + 4 * i for i in range(len(quads)) for b in range(fields))
        if regular:

            @pl.loop(0, len(quads))
            def _(i):
                one_quad(i, lambda b: base[b] + 4 * i)
        else:
            one_quad(0, lambda b: table[0][b])
            later = table[1]

            @pl.loop(1, len(quads))
            def _(i):
                one_quad(i, lambda b: later[b] + 4 * (i - 1))

    for i, quad in enumerate(quads):
        b = 0
        while b < fields:
            source, index = quad[b]
            length = 1
            while b + length < fields and quad[b + length] == (source, index + length):
                length += 1
            target = dyn_ref if source == 0 else trc_ref
            copies.append(
                pltpu.make_async_copy(
                    out_ref.at[pl.ds(i * fields + b, length)],
                    target.at[pl.ds(index, length)],
                    sems.at[len(copies)],
                )
            )
            b += length
    for copy in copies:
        copy.start()
    for copy in copies:
        copy.wait()


def turn(row):
    return jnp.transpose(jnp.broadcast_to(row, (LANES, LANES)))


def route_kernel(devices, owner_ref, counts_ref, position_ref):
    capacity = 2 * 2 * LANES // devices
    owner = owner_ref[...].astype(F32)
    rows = [owner[x : x + 1] for x in range(2)]
    down = [turn(r) for r in rows]
    r, c = row_iota(LANES), lane_iota(LANES)
    ranks = []
    for x in range(2):
        same = jnp.where((down[x] == rows[x]) & (r < c), 1.0, 0.0)
        rank = jnp.sum(same, axis=0, keepdims=True)
        if x == 1:
            rank = rank + jnp.sum(jnp.where(down[0] == rows[1], 1.0, 0.0), axis=0, keepdims=True)
        ranks.append(rank)
        position_ref[0:1, x * LANES : (x + 1) * LANES] = (rows[x] * capacity + rank).astype(jnp.int32)
    device = lax.broadcasted_iota(jnp.int32, (devices, LANES), 0).astype(F32)
    count = sum(
        jnp.sum(jnp.where(device == row, 1.0, 0.0), axis=1, keepdims=True) for row in rows
    )
    counts_ref[...] = jnp.broadcast_to(count[:, :, None], (devices, 1, LANES))


def slot_rows(devices, counts_ref, columns):
    capacity = 2 * columns // devices
    slots = devices * capacity
    counts = jnp.concatenate([counts_ref[d] for d in range(devices)], 0)
    r = lax.broadcasted_iota(jnp.int32, (slots, devices), 0) // capacity
    d = lax.broadcasted_iota(jnp.int32, (slots, devices), 1)
    before = dot(jnp.where(d < r, 1.0, 0.0).astype(BF16), counts.astype(BF16))
    own = dot(jnp.where(d == r, 1.0, 0.0).astype(BF16), counts.astype(BF16))
    rank = (lax.broadcasted_iota(jnp.int32, (slots, LANES), 0) % capacity).astype(F32)
    slot = jnp.where(rank < own, before + rank, -1.0).astype(jnp.int32)
    parts = [
        jnp.where(slot == lane_iota(slots) + LANES * g, 1.0, 0.0) for g in range(columns // LANES)
    ]
    return jnp.concatenate(parts, 1).astype(BF16)


def three_parts(x):
    top = x.astype(BF16)
    rest = x - top.astype(F32)
    mid = rest.astype(BF16)
    return top, mid, (rest - mid.astype(F32)).astype(BF16)


def dot_nt(a, b):
    return lax.dot_general(a, b, (((1,), (1,)), ((), ())), preferred_element_type=F32)


def dot_tn(a, b):
    return lax.dot_general(a, b, (((0,), (0,)), ((), ())), preferred_element_type=F32)


def to_slots(hot, values):
    return sum(dot_nt(hot, part) for part in three_parts(values))


def from_slots(hot, values):
    turned = jnp.transpose(values)
    return sum(dot(part, hot) for part in three_parts(turned))


def pad_rows(x):
    return jnp.concatenate([x, jnp.zeros((LANES - x.shape[0], x.shape[1]), x.dtype)], 0)


def cloud_kernel(devices, counts_ref, cloud_ref, send_ref):
    hot = slot_rows(devices, counts_ref, cloud_ref.shape[1])
    send_ref[...] = to_slots(hot, pad_rows(cloud_ref[...]))


def final_kernel(devices, levels, counts_ref, got_ref, cloud_ref):
    hot = slot_rows(devices, counts_ref, cloud_ref.shape[1])
    cloud_ref[...] = from_slots(hot, got_ref[...])[0:levels]


def physics_kernel(levels, columns_ref, got_ref, position_ref, surface_ref, warm_ref, inc_ref, send_ref, a_ref, g_ref):
    columns = position_ref.shape[1]
    slots = got_ref.shape[0]
    hot = jnp.where(
        position_ref[...] == lax.broadcasted_iota(jnp.int32, (slots, columns), 0), 1.0, 0.0
    ).astype(BF16)
    cloud = from_slots(hot, got_ref[...])[0:levels]
    t, v, c, r = (columns_ref[b, 0:levels, :] for b in range(4))
    surface = surface_ref[...]
    row = lax.broadcasted_iota(jnp.int32, (levels, columns), 0)

    def target_at(s):
        return top_pressure * (1.0 - s) + s * s * surface + s * (1.0 - s) * mid_pressure

    upper = target_at(row.astype(F32) / levels)
    lower = target_at((row + 1).astype(F32) / levels)
    layer = lower - upper
    middle = 0.5 * (lower + upper)
    celsius = 10.0 * t
    saturation = 3.8 / middle * jnp.exp(17.27 * celsius / (celsius + 237.3))
    condensed = jnp.maximum((v - saturation) / (1.0 + kappa_sat * saturation), -c)
    v1 = v - condensed
    c1 = c + condensed
    t1 = t + phase_change_warming * condensed
    converted = c1 * (1.0 - jnp.exp(-(auto_rate * cloud + accrete_rate * r)))
    warm_rows = warm_ref[...]
    warm = jnp.concatenate([warm_rows[0:1], warm_rows[1:2]], 1) == 1
    c2 = jnp.where(warm, c1 - converted, c1)
    r1 = jnp.where(warm, r + converted, r)
    fall = fall_rate * (0.5 + cloud)
    share = 1.0 / (1.0 + fall)
    a_ref[0:levels, :] = r1 * layer
    g_ref[0:levels, :] = fall * share
    held = jnp.zeros((1, columns), F32)
    for k in range(levels):
        held = a_ref[k : k + 1, :] + held
        a_ref[k : k + 1, :] = held
        held = g_ref[k : k + 1, :] * held
    r2 = jnp.where(warm, a_ref[0:levels, :] * share / layer, r1)
    out = flat(inc_ref)
    for b, change in enumerate((t1 - t, v1 - v, c2 - c, r2 - r)):
        for x in range(2):
            out[pl.ds(b * 2 * levels + x, levels, stride=2), :] = change[:, x * LANES : (x + 1) * LANES]
    goal = jnp.clip((v1 / saturation - 0.7) / 0.3, 0.05, 1.0)
    send_ref[...] = to_slots(hot, pad_rows(cloud + 0.5 * (goal - cloud)))


def ring(axis):
    size = lax.axis_size(axis)
    up = [(i, (i + 1) % size) for i in range(size)]
    return up, [(j, i) for i, j in up]


def shape(*dims, dtype=F32):
    return jax.ShapeDtypeStruct(dims, dtype)


def local(dynamics, tracers, thickness, area_weight, cloud_frac, owner, warm_mask):
    levels = thickness.shape[0]
    ndyn, ntrc = dynamics.shape[0], tracers.shape[0]
    nfields = ndyn + ntrc
    rows = -(-(levels + 1) // 8) * 8
    columns = 2 * LANES
    devices = lax.axis_size(("gx", "gy"))
    slots = devices * (2 * columns // devices)
    axes = ("gx", "gy")
    fields = [(0, i) for i in range(1, ndyn)] + [(1, i) for i in range(3, ntrc)]
    quads = [fields[i : i + 4] for i in range(0, len(fields), 4)]
    first_quad = [(0, 0), (1, 0), (1, 1), (1, 2)]
    chunks = [quads[:4], quads[4:]]
    matrix = pack_matrix()
    m = jnp.asarray(matrix, BF16)
    mt = jnp.asarray(matrix.T, BF16)
    mw = jnp.asarray(weight_matrix(), BF16)
    up, down = ring("gx")
    right, left = ring("gy")

    counts, position = pl.pallas_call(
        lambda *refs: route_kernel(devices, *refs),
        out_shape=(shape(devices, 1, LANES), shape(1, columns, dtype=jnp.int32)),
        in_specs=[VM],
        out_specs=(VM, VM),
        compiler_params=params(),
        cost_estimate=cost(1),
        name="route",
    )(owner)
    counts_in = lax.all_to_all(counts, axes, split_axis=0, concat_axis=0, tiled=True)

    up0, down0, edges = pl.pallas_call(
        lambda *refs: first_kernel(levels, first_quad, ndyn, ntrc, *refs),
        out_shape=(shape(TYPES + 1, rows, LANES),) * 2 + (shape(2, rows, LANES),),
        in_specs=[VM] * 6,
        out_specs=(VM,) * 3,
        compiler_params=params(),
        cost_estimate=cost(4),
        name="first_pack",
    )(dynamics, tracers, thickness, area_weight, m, mw)
    before = lax.ppermute(edges, "gy", right)
    after = lax.ppermute(edges, "gy", left)
    from_up0 = lax.ppermute(up0, "gx", up)
    from_down0 = lax.ppermute(down0, "gx", down)

    packed = pl.pallas_call(
        lambda *refs: pack_kernel(levels, chunks, *refs),
        out_shape=tuple(shape(TYPES * len(c), rows, LANES) for c in chunks for _ in range(2)),
        in_specs=[VM] * 5,
        out_specs=(VM,) * (2 * len(chunks)),
        compiler_params=params(),
        cost_estimate=cost(6),
        name="pack",
    )(dynamics, tracers, thickness, area_weight, m)

    row0, row1 = pl.pallas_call(
        edge_kernel,
        out_shape=(shape(rows, LANES),) * 2,
        in_specs=[VM] * 3,
        out_specs=(VM,) * 2,
        compiler_params=params(),
        cost_estimate=cost(1),
        name="edge_sum",
    )(edges, before, after)
    edge_up = lax.ppermute(row1, "gx", up)
    edge_down = lax.ppermute(row0, "gx", down)

    cloud_out = pl.pallas_call(
        lambda *refs: cloud_kernel(devices, *refs),
        out_shape=shape(slots, LANES),
        in_specs=[VM] * 2,
        out_specs=VM,
        compiler_params=params(),
        cost_estimate=cost(2),
        name="cloud_send",
    )(counts_in, cloud_frac)
    cloud_in = lax.all_to_all(cloud_out, axes, split_axis=0, concat_axis=0, tiled=True)

    received = []
    for number in range(len(chunks)):
        received.append(
            (
                lax.ppermute(packed[2 * number], "gx", up),
                lax.ppermute(packed[2 * number + 1], "gx", down),
            )
        )

    weights, indices, edge_values, surface = pl.pallas_call(
        lambda *refs: setup_kernel(levels, nfields, *refs),
        out_shape=(
            shape(2 * TYPES, PARAMS, rows, LANES),
            shape(2 * TYPES, 2, rows, LANES, dtype=jnp.int32),
            shape(2, rows, LANES),
            shape(1, columns),
        ),
        in_specs=[VM] * 8,
        out_specs=(VM,) * 4,
        scratch_shapes=[pltpu.VMEM((3, rows + 16, LANES), F32)],
        compiler_params=params(),
        cost_estimate=cost(5),
        name="column_setup",
    )(down0, up0, from_up0, from_down0, row0, row1, edge_up, edge_down)

    def remap(chunk, own0, own1, got_up, got_down, so_far):
        aliased = so_far is not None
        out_shape = (shape(*dynamics.shape), shape(*tracers.shape))
        args = [own0, own1, got_up, got_down, weights, indices, edge_values, mt]
        in_specs = [VM] * 8
        out_specs = (ANY, ANY)
        aliases = {}
        if aliased:
            args += list(so_far)
            in_specs += [ANY, ANY]
            aliases = {8: 0, 9: 1}
        else:
            out_shape += (shape(4, rows, columns),)
            out_specs += (VM,)
        return pl.pallas_call(
            lambda *refs: remap_kernel(levels, chunk, aliased, *refs),
            out_shape=out_shape,
            in_specs=in_specs,
            out_specs=out_specs,
            input_output_aliases=aliases,
            scratch_shapes=[
                pltpu.VMEM((2, 3, rows + 16, LANES), F32),
                pltpu.VMEM((2 * rows, TYPES * LANES), F32),
                pltpu.VMEM((4 * len(chunk), levels, 2, LANES), F32),
                pltpu.SemaphoreType.DMA((2 * len(chunk),)),
            ],
            compiler_params=params(),
            cost_estimate=cost(4 * len(chunk)),
            name="remap",
        )(*args)

    dyn_new, trc_new, physics_columns = remap([first_quad], down0, up0, from_up0, from_down0, None)

    increments, next_out = pl.pallas_call(
        lambda *refs: physics_kernel(levels, *refs),
        out_shape=(shape(4, levels, 2, LANES), shape(slots, LANES)),
        in_specs=[VM] * 5,
        out_specs=(VM,) * 2,
        scratch_shapes=[pltpu.VMEM((rows, columns), F32)] * 2,
        compiler_params=params(),
        cost_estimate=cost(5),
        name="physics",
    )(physics_columns, cloud_in, position, surface, warm_mask)
    next_in = lax.all_to_all(next_out, axes, split_axis=0, concat_axis=0, tiled=True)

    done = (dyn_new, trc_new)
    for number, chunk in enumerate(chunks):
        done = remap(chunk, packed[2 * number + 1], packed[2 * number], *received[number], done)

    cloud_next = pl.pallas_call(
        lambda *refs: final_kernel(devices, levels, *refs),
        out_shape=shape(levels, columns),
        in_specs=[VM] * 2,
        out_specs=VM,
        compiler_params=params(),
        cost_estimate=cost(2),
        name="cloud_receive",
    )(counts_in, next_in)
    return (done[0], done[1], increments, cloud_next)


def solution(mesh):
    placed = (
        P(None, None, "gx", "gy"),
        P(None, None, "gx", "gy"),
        P(None, "gx", "gy"),
        P("gx", "gy"),
        P(None, ("gx", "gy")),
        P("gx", "gy"),
        P("gx", "gy"),
    )
    return jax.shard_map(
        local,
        mesh=mesh,
        in_specs=placed,
        out_specs=(
            P(None, None, "gx", "gy"),
            P(None, None, "gx", "gy"),
            P(None, None, "gx", "gy"),
            P(None, ("gx", "gy")),
        ),
        check_vma=False,
    )
```

```python
import numpy as np
import jax
import jax.numpy as jnp
from jax import lax
from jax.experimental import pallas as pl
from jax.experimental.pallas import tpu as pltpu
from jax.sharding import PartitionSpec as P

NP = 4
top_pressure = 0.002
mid_pressure = 0.6
kappa_sat = 0.06
phase_change_warming = 0.25
auto_rate = 0.8
accrete_rate = 0.5
fall_rate = 20.0
THICK_MIN = 0.005376344
THICK_MAX = 0.017204301

LANES = 128
BIG = 60
LATE_MB = 24
EARLY = 0.01
HALF = LANES // 2
PART = LANES // NP
TYPES = NP - 1
CHUNKS = (3, 1, 4, 1)
PARAMS = 6
VM = pl.BlockSpec(memory_space=pltpu.VMEM)
ANY = pl.BlockSpec(memory_space=pl.ANY)
F32 = jnp.float32
BF16 = jnp.bfloat16


def params(vmem=LATE_MB):
    return pltpu.CompilerParams(vmem_limit_bytes=vmem * 1024 * 1024)


def cost(us):
    return pl.CostEstimate(flops=int(us * 1.0e9), bytes_accessed=int(us * 3.0e6), transcendentals=0)


def source_windows(levels):
    slack = 1e-4
    lo, hi = THICK_MIN * (1 - slack), THICK_MAX * (1 + slack)
    k = np.arange(levels)
    surfaces = np.linspace(top_pressure + levels * lo, top_pressure + levels * hi, 4001)[:, None]
    least = np.maximum(top_pressure + lo * k, surfaces - hi * (levels - k))
    most = np.minimum(top_pressure + hi * k, surfaces - lo * (levels - k))
    out = []
    for t in range(1, levels + 1):
        s = t / levels
        p = top_pressure * (1 - s) + s * s * surfaces + s * (1 - s) * mid_pressure
        first = np.min(np.sum(most <= p, axis=1)) - 1
        last = np.max(np.sum(least <= p, axis=1)) - 1
        out.append((max(int(first) - 1, 0), min(int(last) + 1, levels - 1)))
    return out


def tile_windows(levels):
    per_edge = source_windows(levels)
    tiles = -(-levels // 8)
    out = []
    for j in range(tiles):
        rows = per_edge[8 * j : min(8 * j + 8, levels)]
        out.append((min(r[0] for r in rows), max(r[1] for r in rows)))
    return out


def pack_matrix():
    m = np.zeros((NP * LANES, TYPES * LANES), np.float32)
    for b in range(NP):
        for e in range(PART):
            m[b * LANES + NP * e, b * PART + e] = 1
            if e:
                m[b * LANES + NP * e - 1, b * PART + e] = 1
            m[b * LANES + NP * e + 1, LANES + b * PART + e] = 1
            m[b * LANES + NP * e + 2, 2 * LANES + b * PART + e] = 1
    return m


def weight_matrix():
    m = np.zeros((LANES, LANES), np.float32)
    for e in range(PART):
        for base in (0, 3 * PART):
            m[NP * e, base + e] = 1
            if e:
                m[NP * e - 1, base + e] = 1
        m[NP * e + 1, PART + e] = 1
        m[NP * e + 2, 2 * PART + e] = 1
    return m


def split2(x):
    top = x.astype(BF16)
    return top, (x - top.astype(F32)).astype(BF16)


def dot(a, b):
    return jnp.dot(a, b, preferred_element_type=F32)


def select_dot2(x, m):
    rows = x.shape[0]
    top, low = split2(x)
    return dot(top, m) + dot(low, m)


def select_dot3(x, m):
    top = x.astype(BF16)
    rest = x - top.astype(F32)
    mid = rest.astype(BF16)
    low = (rest - mid.astype(F32)).astype(BF16)
    return dot(top, m) + dot(mid, m) + dot(low, m)


def lane_iota(rows):
    return lax.broadcasted_iota(jnp.int32, (rows, LANES), 1)


def row_iota(rows):
    return lax.broadcasted_iota(jnp.int32, (rows, LANES), 0)


def pick_lanes(x, index):
    return jnp.take_along_axis(x, index, axis=1, mode="promise_in_bounds")


def prefix_rows(x):
    tiles = x.shape[0] // 8
    row = row_iota(8)
    carry = jnp.zeros((8, LANES), F32)
    out = []
    for j in range(tiles):
        part = x[8 * j : 8 * j + 8]
        for step in (1, 2, 4):
            part = part + jnp.where(row >= step, pltpu.roll(part, step, 0), 0.0)
        part = part + carry
        carry = jnp.broadcast_to(part[7:8], (8, LANES))
        out.append(part)
    return jnp.concatenate(out, 0)


def field_rows(dyn, trc, levels, which, x):
    source, index = which
    ref = dyn if source == 0 else trc
    return ref[pl.ds(index * 2 * levels + x, levels, stride=2), :]


def pack_quad(dyn, trc, weight, m, quad, x, levels):
    rows = jnp.concatenate(
        [weight[x] * field_rows(dyn, trc, levels, which, x) for which in quad], 1
    )
    return select_dot2(rows, m)


def flat(ref):
    lead = 1
    for size in ref.shape[:-1]:
        lead *= size
    return ref.reshape(lead, LANES)


def runs_of(fields):
    runs = []
    for source, index in fields:
        if runs and runs[-1][0] == source and runs[-1][1] + runs[-1][2] == index:
            runs[-1][2] += 1
        else:
            runs.append([source, index, 1])
    return runs


def start_loads(quads, dyn_hbm, trc_hbm, buffer, sems):
    loads, b, count = [], 0, 0
    for quad in quads:
        copies = []
        for source, index, length in runs_of(quad):
            ref = dyn_hbm if source == 0 else trc_hbm
            copies.append(
                pltpu.make_async_copy(
                    ref.at[pl.ds(index, length)], buffer.at[pl.ds(b, length)], sems.at[count]
                )
            )
            b, count = b + length, count + 1
        for copy in copies:
            copy.start()
        loads.append(copies)
    return loads


def pack_kernel(levels, chunks, weights_too, dyn_hbm, trc_hbm, thick3, area_ref, m_ref, *rest):
    buffer, sems = rest[-2:]
    outs = rest[-2 - 2 * len(chunks) : -2]
    rest = rest[: -2 - 2 * len(chunks)]
    quads = [quad for chunk in chunks for quad in chunk]
    loads = start_loads(quads, dyn_hbm, trc_hbm, buffer, sems)
    fields, thick = flat(buffer), flat(thick3)
    weight = [area_ref[x : x + 1, :] * thick[pl.ds(x, levels, stride=2), :] for x in range(2)]
    m = m_ref[...]
    last = TYPES * len(chunks[0])
    if weights_too:
        mw_ref = rest[0]
        for x, out in ((0, outs[1]), (1, outs[0])):
            out[last, 0:levels, :] = select_dot3(weight[x], mw_ref[...])
            area = jnp.broadcast_to(area_ref[x : x + 1, :], (8, LANES))
            out[last, levels : levels + 1, :] = select_dot3(area, mw_ref[...])[0:1]
    if len(rest) == 4:
        own_ref, before_ref, after_ref = rest[:3]
        left = lane_iota(own_ref.shape[1]) < HALF
        for x, out in ((0, outs[1]), (1, outs[0])):
            out[last] = own_ref[x] + jnp.where(
                left, pltpu.roll(before_ref[x], HALF, 1), pltpu.roll(after_ref[x], HALF, 1)
            )
    number = 0
    for place, chunk in enumerate(chunks):
        for i in range(len(chunk)):
            for copy in loads[number]:
                copy.wait()
            where = [(1, NP * number + b) for b in range(NP)]
            for x, out in ((0, outs[2 * place + 1]), (1, outs[2 * place])):
                packed = pack_quad(None, fields, weight, m, where, x, levels)
                for kind in range(TYPES):
                    out[TYPES * i + kind, 0:levels, :] = packed[:, kind * LANES : (kind + 1) * LANES]
            number += 1


def ends_kernel(levels, ndyn, ntrc, dyn_hbm, trc_hbm, thick3, area_ref, after_ref, edge_ref, buffer, sems):
    groups = [[(0, i) for i in range(ndyn)]]
    groups += [[(1, i) for i in range(k, min(k + 11, ntrc))] for k in range(0, ntrc, 11)]
    loads = start_loads(groups, dyn_hbm, trc_hbm, buffer, sems)
    rows, thick = flat(buffer), flat(thick3)
    weight = [area_ref[x : x + 1, :] * thick[pl.ds(x, levels, stride=2), :] for x in range(2)]
    lane = lane_iota(levels)
    ends = jnp.where(lane < HALF, 0, LANES - 1)
    spot = lane % HALF
    count = ndyn + ntrc
    totals = [jnp.zeros((levels, LANES), F32)] * 2
    number = 0
    for group, copies in zip(groups, loads):
        for copy in copies:
            copy.wait()
        for _ in group:
            for x in range(2):
                here = pick_lanes(field_rows(None, rows, levels, (1, number), x), ends)
                totals[x] = jnp.where(spot == number, here, totals[x])
            number += 1
    for x in range(2):
        both = pick_lanes(weight[x], ends)
        edge_ref[x, 0:levels, :] = jnp.where(spot == count, 1.0, totals[x]) * both
        edge_ref[x, levels : levels + 1, :] = pick_lanes(
            jnp.broadcast_to(area_ref[x : x + 1, :], (8, LANES)), ends[0:8]
        )[0:1]


def remap_group(levels, windows, summed, rm, thick, al, ar, aq, rdt, tile_of, row_of, s_ref):
    rows = summed.shape[0]
    tiles = rows // 8
    q = summed * rm
    first = q[0:1]
    last = jnp.broadcast_to(q[levels - 1 : levels], (rows - levels + 2, LANES))
    s_ref[0, 8 : 8 + rows, :] = q
    s_ref[0, 7:8, :] = first
    s_ref[0, 8 + levels : 10 + rows, :] = last
    below = s_ref[0, 7 : 7 + rows, :]
    q = s_ref[0, 8 : 8 + rows, :]
    above = s_ref[0, 9 : 9 + rows, :]
    above_two = s_ref[0, 10 : 10 + rows, :]
    edge = 7.0 / 12.0 * (q + above) - 1.0 / 12.0 * (below + above_two)
    edge = jnp.clip(edge, jnp.minimum(q, above), jnp.maximum(q, above))
    s_ref[1, 8 : 8 + rows, :] = edge
    s_ref[1, 7:8, :] = first
    left = s_ref[1, 7 : 7 + rows, :]
    layer = thick * q
    through = prefix_rows(layer) - layer
    for j in range(tiles):
        low, high = windows[j][0] // 8, windows[j][1] // 8
        part = slice(8 * j, 8 * j + 8)
        tile, row = tile_of[part], row_of[part]
        got = None
        for v in range(low, high + 1):
            here = [
                jnp.take_along_axis(a[8 * v : 8 * v + 8], row, axis=0, mode="promise_in_bounds")
                for a in (through, left, edge, q)
            ]
            if got is None:
                got = here
            else:
                got = [jnp.where(tile == v, new, old) for new, old in zip(here, got)]
        s_ref[2, 8 + 8 * j : 16 + 8 * j, :] = (
            got[0] + al[part] * got[1] + ar[part] * got[2] + aq[part] * got[3]
        )
    s_ref[2, 7:8, :] = jnp.zeros((1, LANES), F32)
    return (s_ref[2, 8 : 8 + rows, :] - s_ref[2, 7 : 7 + rows, :]) * rdt


def column_surface(weights_surface, edge_surface):
    lane = lane_iota(8)
    spot, kind = lane // NP, lane % NP
    index = jnp.where(kind == 3, jnp.minimum(spot + 1, PART - 1), kind * PART + spot)
    inner = pick_lanes(weights_surface, index)
    return jnp.where((lane == 0) | (lane == LANES - 1), edge_surface, inner)


def setup_kernel(levels, nfields, own0, own1, from_up, from_down, row0, row1, edge_up, edge_down, p_ref, i_ref, e_ref, surface_ref, s_ref):
    windows = tile_windows(levels)
    rows = row0.shape[1]
    tiles = rows // 8
    row = row_iota(rows)
    lane = lane_iota(rows)
    inside = row < levels
    edge_lanes = jnp.where(lane < HALF, nfields, HALF + nfields)
    kept = []
    for base in range(4):
        x = base % 2
        own, got = ((own0, from_up), (own1, from_down))[x]
        eown, egot = ((row0, edge_up), (row1, edge_down))[x]
        if base < 2:
            mass = own[0] + got[0]
        else:
            summed = eown[0] + egot[0]
            mass = pick_lanes(summed, edge_lanes)
        area = mass[levels : levels + 1]
        mass = jnp.where(inside, mass, 1.0)
        thick = jnp.where(inside, mass / area, 1.0)
        after = top_pressure + prefix_rows(thick)
        surface = after[levels - 1 : levels]
        s_ref[0, 8 : 8 + rows, :] = after
        s_ref[0, 7:8, :] = jnp.full((1, LANES), top_pressure, F32)
        s_ref[1, 0:rows, :] = thick
        sigma = (row + 1).astype(F32) / levels
        sigma0 = row.astype(F32) / levels

        def target_at(s):
            return top_pressure * (1.0 - s) + s * s * surface + s * (1.0 - s) * mid_pressure

        target = target_at(sigma)
        rdt = jnp.where(inside, 1.0 / (target - target_at(sigma0)), 1.0)
        index, start, depth = [], [], []
        for j in range(tiles):
            low, high = windows[j]
            here = target[8 * j : 8 * j + 8]
            count = jnp.full((8, LANES), low, jnp.int32)
            source = jnp.broadcast_to(s_ref[0, 7 + low : 8 + low, :], (8, LANES))
            size = jnp.broadcast_to(s_ref[1, low : low + 1, :], (8, LANES))
            for k in range(low + 1, high + 1):
                edge_k = jnp.broadcast_to(s_ref[0, 7 + k : 8 + k, :], (8, LANES))
                size_k = jnp.broadcast_to(s_ref[1, k : k + 1, :], (8, LANES))
                reached = edge_k <= here
                count = jnp.where(reached, k, count)
                source = jnp.where(reached, edge_k, source)
                size = jnp.where(reached, size_k, size)
            index.append(count)
            start.append(source)
            depth.append(size)
        index, start, depth = (jnp.concatenate(a, 0) for a in (index, start, depth))
        f = jnp.clip((target - start) / depth, 0.0, 1.0)
        f2, f3 = f * f, f * f * f
        values = [
            1.0 / mass,
            thick,
            depth * (f - 2.0 * f2 + f3),
            depth * (f3 - f2),
            depth * (3.0 * f2 - 2.0 * f3),
            rdt,
        ]
        tile_of, row_of = index >> 3, index & 7
        if base < 2:
            for kind in range(TYPES):
                lanes = kind * PART + lane % PART
                group = 2 * kind + x
                for i, value in enumerate(values):
                    p_ref[group, i] = pick_lanes(value, lanes)
                i_ref[group, 0] = pick_lanes(tile_of, lanes)
                i_ref[group, 1] = pick_lanes(row_of, lanes)
            kept.append(jnp.broadcast_to(surface, (8, LANES)))
        else:
            e_ref[x] = remap_group(levels, windows, summed, *values, tile_of, row_of, s_ref)
            surface_ref[0:1, x * LANES : (x + 1) * LANES] = column_surface(
                kept[x], jnp.broadcast_to(surface, (8, LANES))
            )[0:1]


def remap_kernel(levels, ndyn, quads, aliased, extra, own0, own1, from_up, from_down, p_ref, i_ref, e_ref, mt_ref, *rest):
    if aliased:
        rest = rest[2 + extra :]
        dyn_ref, trc_ref = rest[:2]
        columns_ref = None
        rest = rest[2:]
    else:
        dyn_ref, trc_ref, columns_ref = rest[:3]
        rest = rest[3:]
    s_ref, packed_ref, out_ref, sems = rest
    windows = tile_windows(levels)
    rows = e_ref.shape[1]
    lane = lane_iota(levels)
    ends = (lane == 0) | (lane == LANES - 1)
    half = jnp.where(lane < HALF, 0, HALF)
    out_rows = flat(out_ref)
    fields = TYPES + 1

    def one_quad(i, edge_lane):
        for kind in range(TYPES):
            for x in range(2):
                group = 2 * kind + x
                own, got = ((own0, from_up), (own1, from_down))[x]
                summed = own[TYPES * i + kind] + got[TYPES * i + kind]
                values = [p_ref[group, n] for n in range(PARAMS)]
                packed_ref[x * rows : (x + 1) * rows, kind * LANES : (kind + 1) * LANES] = remap_group(
                    levels, windows, summed, *values, i_ref[group, 0], i_ref[group, 1], s_ref.at[x]
                )
        wide = select_dot2(packed_ref[...], mt_ref[...])
        for b in range(fields):
            for x in range(2):
                value = wide[x * rows : x * rows + levels, b * LANES : (b + 1) * LANES]
                outer = pick_lanes(e_ref[x, 0:levels, :], half + edge_lane(b))
                value = jnp.where(ends, outer, value)
                out_rows[pl.ds((i * fields + b) * 2 * levels + x, levels, stride=2), :] = value
                if columns_ref is not None and isinstance(i, int) and i == 0:
                    columns_ref[b, 0:levels, x * LANES : (x + 1) * LANES] = value

    table = [[index + (0 if source == 0 else ndyn) for source, index in quad] for quad in quads]
    start = len(quads) - 1 if aliased else max(len(quads) - 1, 1)
    while start > 1 and table[start] == [v + fields for v in table[start - 1]]:
        start -= 1
    for i in range(start):
        one_quad(i, lambda b: table[i][b])

    @pl.loop(start, len(quads))
    def _(i):
        one_quad(i, lambda b: table[start][b] + fields * (i - start))

    copies = []
    for i, quad in enumerate(quads):
        b = 0
        while b < fields:
            source, index = quad[b]
            length = 1
            while b + length < fields and quad[b + length] == (source, index + length):
                length += 1
            target = dyn_ref if source == 0 else trc_ref
            copies.append(
                pltpu.make_async_copy(
                    out_ref.at[pl.ds(i * fields + b, length)],
                    target.at[pl.ds(index, length)],
                    sems.at[len(copies)],
                )
            )
            b += length
    for copy in copies:
        copy.start()
    for copy in copies:
        copy.wait()


def turn(row):
    return jnp.transpose(jnp.broadcast_to(row, (LANES, LANES)))


def route_kernel(devices, owner_ref, counts_ref, position_ref):
    capacity = 2 * 2 * LANES // devices
    owner = owner_ref[...].astype(F32)
    rows = [owner[x : x + 1] for x in range(2)]
    down = [turn(r) for r in rows]
    r, c = row_iota(LANES), lane_iota(LANES)
    ranks = []
    for x in range(2):
        same = jnp.where((down[x] == rows[x]) & (r < c), 1.0, 0.0)
        rank = jnp.sum(same, axis=0, keepdims=True)
        if x == 1:
            rank = rank + jnp.sum(jnp.where(down[0] == rows[1], 1.0, 0.0), axis=0, keepdims=True)
        ranks.append(rank)
        position_ref[0:1, x * LANES : (x + 1) * LANES] = (rows[x] * capacity + rank).astype(jnp.int32)
    device = lax.broadcasted_iota(jnp.int32, (devices, LANES), 0).astype(F32)
    count = sum(
        jnp.sum(jnp.where(device == row, 1.0, 0.0), axis=1, keepdims=True) for row in rows
    )
    counts_ref[...] = jnp.broadcast_to(count[:, :, None], (devices, 1, LANES))


def slot_rows(devices, counts_ref, columns):
    capacity = 2 * columns // devices
    slots = devices * capacity
    counts = jnp.concatenate([counts_ref[d] for d in range(devices)], 0)
    r = lax.broadcasted_iota(jnp.int32, (slots, devices), 0) // capacity
    d = lax.broadcasted_iota(jnp.int32, (slots, devices), 1)
    before = dot(jnp.where(d < r, 1.0, 0.0).astype(BF16), counts.astype(BF16))
    own = dot(jnp.where(d == r, 1.0, 0.0).astype(BF16), counts.astype(BF16))
    rank = (lax.broadcasted_iota(jnp.int32, (slots, LANES), 0) % capacity).astype(F32)
    slot = jnp.where(rank < own, before + rank, -1.0).astype(jnp.int32)
    parts = [
        jnp.where(slot == lane_iota(slots) + LANES * g, 1.0, 0.0) for g in range(columns // LANES)
    ]
    return jnp.concatenate(parts, 1).astype(BF16)


def three_parts(x):
    top = x.astype(BF16)
    rest = x - top.astype(F32)
    mid = rest.astype(BF16)
    return top, mid, (rest - mid.astype(F32)).astype(BF16)


def dot_nt(a, b):
    return lax.dot_general(a, b, (((1,), (1,)), ((), ())), preferred_element_type=F32)


def dot_tn(a, b):
    return lax.dot_general(a, b, (((0,), (0,)), ((), ())), preferred_element_type=F32)


def to_slots(hot, values):
    return sum(dot_nt(hot, part) for part in three_parts(values))


def from_slots(hot, values):
    turned = jnp.transpose(values)
    return sum(dot(part, hot) for part in three_parts(turned))


def pad_rows(x):
    return jnp.concatenate([x, jnp.zeros((LANES - x.shape[0], x.shape[1]), x.dtype)], 0)


def cloud_kernel(devices, counts_ref, cloud_ref, *rest):
    send_ref = rest[-1]
    hot = slot_rows(devices, counts_ref, cloud_ref.shape[1])
    send_ref[...] = to_slots(hot, pad_rows(cloud_ref[...]))


def final_kernel(devices, levels, counts_ref, got_ref, cloud_ref):
    hot = slot_rows(devices, counts_ref, cloud_ref.shape[1])
    cloud_ref[...] = from_slots(hot, got_ref[...])[0:levels]


def physics_kernel(levels, columns_ref, got_ref, position_ref, surface_ref, warm_ref, inc_ref, send_ref, a_ref, g_ref):
    columns = position_ref.shape[1]
    slots = got_ref.shape[0]
    hot = jnp.where(
        position_ref[...] == lax.broadcasted_iota(jnp.int32, (slots, columns), 0), 1.0, 0.0
    ).astype(BF16)
    cloud = from_slots(hot, got_ref[...])[0:levels]
    t, v, c, r = (columns_ref[b, 0:levels, :] for b in range(4))
    surface = surface_ref[...]
    row = lax.broadcasted_iota(jnp.int32, (levels, columns), 0)

    def target_at(s):
        return top_pressure * (1.0 - s) + s * s * surface + s * (1.0 - s) * mid_pressure

    upper = target_at(row.astype(F32) / levels)
    lower = target_at((row + 1).astype(F32) / levels)
    layer = lower - upper
    middle = 0.5 * (lower + upper)
    celsius = 10.0 * t
    saturation = 3.8 / middle * jnp.exp(17.27 * celsius / (celsius + 237.3))
    condensed = jnp.maximum((v - saturation) / (1.0 + kappa_sat * saturation), -c)
    v1 = v - condensed
    c1 = c + condensed
    t1 = t + phase_change_warming * condensed
    converted = c1 * (1.0 - jnp.exp(-(auto_rate * cloud + accrete_rate * r)))
    warm_rows = warm_ref[...]
    warm = jnp.concatenate([warm_rows[0:1], warm_rows[1:2]], 1) == 1
    c2 = jnp.where(warm, c1 - converted, c1)
    r1 = jnp.where(warm, r + converted, r)
    fall = fall_rate * (0.5 + cloud)
    share = 1.0 / (1.0 + fall)
    a_ref[0:levels, :] = r1 * layer
    g_ref[0:levels, :] = fall * share
    held = jnp.zeros((1, columns), F32)
    for k in range(levels):
        held = a_ref[k : k + 1, :] + held
        a_ref[k : k + 1, :] = held
        held = g_ref[k : k + 1, :] * held
    r2 = jnp.where(warm, a_ref[0:levels, :] * share / layer, r1)
    out = flat(inc_ref)
    for b, change in enumerate((t1 - t, v1 - v, c2 - c, r2 - r)):
        for x in range(2):
            out[pl.ds(b * 2 * levels + x, levels, stride=2), :] = change[:, x * LANES : (x + 1) * LANES]
    goal = jnp.clip((v1 / saturation - 0.7) / 0.3, 0.05, 1.0)
    send_ref[...] = to_slots(hot, pad_rows(cloud + 0.5 * (goal - cloud)))


def ring(axis):
    size = lax.axis_size(axis)
    up = [(i, (i + 1) % size) for i in range(size)]
    return up, [(j, i) for i, j in up]


def shape(*dims, dtype=F32):
    return jax.ShapeDtypeStruct(dims, dtype)


def local(dynamics, tracers, thickness, area_weight, cloud_frac, owner, warm_mask):
    levels = thickness.shape[0]
    ndyn, ntrc = dynamics.shape[0], tracers.shape[0]
    nfields = ndyn + ntrc
    rows = -(-(levels + 1) // 8) * 8
    columns = 2 * LANES
    devices = lax.axis_size(("gx", "gy"))
    slots = devices * (2 * columns // devices)
    axes = ("gx", "gy")
    fields = [(0, i) for i in range(1, ndyn)] + [(1, i) for i in range(3, ntrc)]
    quads = [fields[i : i + 4] for i in range(0, len(fields), 4)]
    first_quad = [(0, 0), (1, 0), (1, 1), (1, 2)]
    quads = [first_quad] + quads
    chunks, begin = [], 0
    for length in CHUNKS:
        chunks.append(quads[begin : begin + length])
        begin += length
    assert begin == len(quads)
    matrix = pack_matrix()
    m = jnp.asarray(matrix, BF16)
    mt = jnp.asarray(matrix.T, BF16)
    mw = jnp.asarray(weight_matrix(), BF16)
    up, down = ring("gx")
    right, left = ring("gy")
    fields_in = (dynamics, tracers, thickness, area_weight)

    packed, received = [None] * len(chunks), [None] * len(chunks)

    def send(numbers, extra, args, specs, name):
        parts = [chunks[n] for n in numbers]
        total = sum(len(part) for part in parts)
        sent = pl.pallas_call(
            lambda *refs: pack_kernel(levels, parts, numbers[0] == 0, *refs),
            out_shape=tuple(
                shape(TYPES * len(part) + extra, rows, LANES) for part in parts for _ in range(2)
            ),
            in_specs=[ANY, ANY] + [VM] * 3 + specs,
            out_specs=(VM,) * (2 * len(parts)),
            scratch_shapes=[
                pltpu.VMEM((NP * total, levels, 2, LANES), F32),
                pltpu.SemaphoreType.DMA((2 * total,)),
            ],
            compiler_params=params(BIG),
            cost_estimate=cost(EARLY),
            name=name,
        )(*fields_in, m, *args)
        for i, n in enumerate(numbers):
            packed[n] = (sent[2 * i], sent[2 * i + 1])
            received[n] = (
                lax.ppermute(sent[2 * i], "gx", up),
                lax.ppermute(sent[2 * i + 1], "gx", down),
            )

    counts, position = pl.pallas_call(
        lambda *refs: route_kernel(devices, *refs),
        out_shape=(shape(devices, 1, LANES), shape(1, columns, dtype=jnp.int32)),
        in_specs=[VM],
        out_specs=(VM, VM),
        compiler_params=params(BIG),
        cost_estimate=cost(EARLY),
        name="route",
    )(owner)
    counts_in = lax.all_to_all(counts, axes, split_axis=0, concat_axis=0, tiled=True)

    send([0], 1, (mw, counts), [VM, ANY], "first_pack")

    edges = pl.pallas_call(
        lambda *refs: ends_kernel(levels, ndyn, ntrc, *refs),
        out_shape=shape(2, rows, LANES),
        in_specs=[ANY, ANY, VM, VM, ANY],
        out_specs=VM,
        scratch_shapes=[
            pltpu.VMEM((nfields, levels, 2, LANES), F32),
            pltpu.SemaphoreType.DMA((8,)),
        ],
        compiler_params=params(BIG),
        cost_estimate=cost(EARLY),
        name="ends",
    )(*fields_in, packed[0][0])
    before = lax.ppermute(edges, "gy", right)
    after = lax.ppermute(edges, "gy", left)

    cloud_out = pl.pallas_call(
        lambda *refs: cloud_kernel(devices, *refs),
        out_shape=shape(slots, LANES),
        in_specs=[VM] * 2 + [ANY] * 3,
        out_specs=VM,
        compiler_params=params(),
        cost_estimate=cost(2),
        name="cloud_send",
    )(counts_in, cloud_frac, packed[0][0], *received[0])
    cloud_in = lax.all_to_all(cloud_out, axes, split_axis=0, concat_axis=0, tiled=True)

    send([1], 1, (edges, before, after, cloud_out), [VM] * 3 + [ANY], "second_pack")

    send(list(range(2, len(chunks))), 0, (packed[1][0],), [ANY], "pack")
    def one_group(number):
        group = TYPES * len(chunks[number])
        return pl.BlockSpec((1, rows, LANES), lambda i: (group, 0, 0))

    def full(*dims):
        return pl.BlockSpec(dims, lambda i: (0,) * len(dims))

    weights, indices, edge_values, surface = pl.pallas_call(
        lambda *refs: setup_kernel(levels, nfields, *refs),
        grid=(1,),
        out_shape=(
            shape(2 * TYPES, PARAMS, rows, LANES),
            shape(2 * TYPES, 2, rows, LANES, dtype=jnp.int32),
            shape(2, rows, LANES),
            shape(1, columns),
        ),
        in_specs=[one_group(0)] * 4 + [one_group(1)] * 4,
        out_specs=(
            full(2 * TYPES, PARAMS, rows, LANES),
            full(2 * TYPES, 2, rows, LANES),
            full(2, rows, LANES),
            full(1, columns),
        ),
        scratch_shapes=[pltpu.VMEM((3, rows + 16, LANES), F32)],
        compiler_params=params(BIG),
        cost_estimate=cost(5),
        name="column_setup",
    )(packed[0][1], packed[0][0], *received[0], packed[1][1], packed[1][0], *received[1])

    def remap(chunk, own0, own1, got_up, got_down, so_far, follows=()):
        aliased = so_far is not None
        out_shape = (shape(*dynamics.shape), shape(*tracers.shape))
        args = [own0, own1, got_up, got_down, weights, indices, edge_values, mt]
        in_specs = [VM] * 8
        out_specs = (ANY, ANY)
        aliases = {}
        if aliased:
            args += list(so_far) + list(follows)
            in_specs += [ANY] * (2 + len(follows))
            aliases = {8: 0, 9: 1}
        else:
            out_shape += (shape(4, rows, columns),)
            out_specs += (VM,)
        return pl.pallas_call(
            lambda *refs: remap_kernel(levels, ndyn, chunk, aliased, len(follows), *refs),
            out_shape=out_shape,
            in_specs=in_specs,
            out_specs=out_specs,
            input_output_aliases=aliases,
            scratch_shapes=[
                pltpu.VMEM((2, 3, rows + 16, LANES), F32),
                pltpu.VMEM((2 * rows, TYPES * LANES), F32),
                pltpu.VMEM((4 * len(chunk), levels, 2, LANES), F32),
                pltpu.SemaphoreType.DMA((2 * len(chunk),)),
            ],
            compiler_params=params(),
            cost_estimate=cost(2 * len(chunk)),
            name="remap",
        )(*args)

    dyn_new, trc_new, physics_columns = remap(
        chunks[0], packed[0][1], packed[0][0], *received[0], None
    )

    increments, next_out = pl.pallas_call(
        lambda *refs: physics_kernel(levels, *refs),
        out_shape=(shape(4, levels, 2, LANES), shape(slots, LANES)),
        in_specs=[VM] * 5,
        out_specs=(VM,) * 2,
        scratch_shapes=[pltpu.VMEM((rows, columns), F32)] * 2,
        compiler_params=params(),
        cost_estimate=cost(5),
        name="physics",
    )(physics_columns, cloud_in, position, surface, warm_mask)
    next_in = lax.all_to_all(next_out, axes, split_axis=0, concat_axis=0, tiled=True)

    done = (dyn_new, trc_new)
    for number, chunk in list(enumerate(chunks))[1:]:
        done = remap(chunk, packed[number][1], packed[number][0], *received[number], done, (next_out,) if number > 1 else ())

    cloud_next = pl.pallas_call(
        lambda *refs: final_kernel(devices, levels, *refs),
        out_shape=shape(levels, columns),
        in_specs=[VM] * 2,
        out_specs=VM,
        compiler_params=params(),
        cost_estimate=cost(2),
        name="cloud_receive",
    )(counts_in, next_in)
    return (done[0], done[1], increments, cloud_next)


def solution(mesh):
    placed = (
        P(None, None, "gx", "gy"),
        P(None, None, "gx", "gy"),
        P(None, "gx", "gy"),
        P("gx", "gy"),
        P(None, ("gx", "gy")),
        P("gx", "gy"),
        P("gx", "gy"),
    )
    return jax.shard_map(
        local,
        mesh=mesh,
        in_specs=placed,
        out_specs=(
            P(None, None, "gx", "gy"),
            P(None, None, "gx", "gy"),
            P(None, None, "gx", "gy"),
            P(None, ("gx", "gy")),
        ),
        check_vma=False,
    )
```

```python
import numpy as np
import jax
import jax.numpy as jnp
from jax import lax
from jax.experimental import pallas as pl
from jax.experimental.pallas import tpu as pltpu
from jax.sharding import PartitionSpec as P

NP = 4
top_pressure = 0.002
mid_pressure = 0.6
kappa_sat = 0.06
phase_change_warming = 0.25
auto_rate = 0.8
accrete_rate = 0.5
fall_rate = 20.0
THICK_MIN = 0.005376344
THICK_MAX = 0.017204301

LANES = 128
BIG = 60
LATE_MB = 24
EARLY = 0.01
HALF = LANES // 2
PART = LANES // NP
TYPES = NP - 1
CHUNKS = (3, 1, 3, 2)
PARAMS = 6
VM = pl.BlockSpec(memory_space=pltpu.VMEM)
ANY = pl.BlockSpec(memory_space=pl.ANY)
F32 = jnp.float32
BF16 = jnp.bfloat16


def params(vmem=LATE_MB):
    return pltpu.CompilerParams(vmem_limit_bytes=vmem * 1024 * 1024)


def cost(us):
    return pl.CostEstimate(flops=int(us * 1.0e9), bytes_accessed=int(us * 3.0e6), transcendentals=0)


def source_windows(levels):
    slack = 1e-4
    lo, hi = THICK_MIN * (1 - slack), THICK_MAX * (1 + slack)
    k = np.arange(levels)
    surfaces = np.linspace(top_pressure + levels * lo, top_pressure + levels * hi, 4001)[:, None]
    least = np.maximum(top_pressure + lo * k, surfaces - hi * (levels - k))
    most = np.minimum(top_pressure + hi * k, surfaces - lo * (levels - k))
    out = []
    for t in range(1, levels + 1):
        s = t / levels
        p = top_pressure * (1 - s) + s * s * surfaces + s * (1 - s) * mid_pressure
        first = np.min(np.sum(most <= p, axis=1)) - 1
        last = np.max(np.sum(least <= p, axis=1)) - 1
        out.append((max(int(first) - 1, 0), min(int(last) + 1, levels - 1)))
    return out


def tile_windows(levels):
    per_edge = source_windows(levels)
    tiles = -(-levels // 8)
    out = []
    for j in range(tiles):
        rows = per_edge[8 * j : min(8 * j + 8, levels)]
        out.append((min(r[0] for r in rows), max(r[1] for r in rows)))
    return out


def pack_matrix():
    m = np.zeros((NP * LANES, TYPES * LANES), np.float32)
    for b in range(NP):
        for e in range(PART):
            m[b * LANES + NP * e, b * PART + e] = 1
            if e:
                m[b * LANES + NP * e - 1, b * PART + e] = 1
            m[b * LANES + NP * e + 1, LANES + b * PART + e] = 1
            m[b * LANES + NP * e + 2, 2 * LANES + b * PART + e] = 1
    return m


def weight_matrix():
    m = np.zeros((LANES, LANES), np.float32)
    for e in range(PART):
        for base in (0, 3 * PART):
            m[NP * e, base + e] = 1
            if e:
                m[NP * e - 1, base + e] = 1
        m[NP * e + 1, PART + e] = 1
        m[NP * e + 2, 2 * PART + e] = 1
    return m


def split2(x):
    top = x.astype(BF16)
    return top, (x - top.astype(F32)).astype(BF16)


def dot(a, b):
    return jnp.dot(a, b, preferred_element_type=F32)


def select_dot2(x, m):
    rows = x.shape[0]
    top, low = split2(x)
    return dot(top, m) + dot(low, m)


def select_dot3(x, m):
    top = x.astype(BF16)
    rest = x - top.astype(F32)
    mid = rest.astype(BF16)
    low = (rest - mid.astype(F32)).astype(BF16)
    return dot(top, m) + dot(mid, m) + dot(low, m)


def lane_iota(rows):
    return lax.broadcasted_iota(jnp.int32, (rows, LANES), 1)


def row_iota(rows):
    return lax.broadcasted_iota(jnp.int32, (rows, LANES), 0)


def pick_lanes(x, index):
    return jnp.take_along_axis(x, index, axis=1, mode="promise_in_bounds")


def prefix_rows(x):
    tiles = x.shape[0] // 8
    row = row_iota(8)
    carry = jnp.zeros((8, LANES), F32)
    out = []
    for j in range(tiles):
        part = x[8 * j : 8 * j + 8]
        for step in (1, 2, 4):
            part = part + jnp.where(row >= step, pltpu.roll(part, step, 0), 0.0)
        part = part + carry
        carry = jnp.broadcast_to(part[7:8], (8, LANES))
        out.append(part)
    return jnp.concatenate(out, 0)


def field_rows(dyn, trc, levels, which, x):
    source, index = which
    ref = dyn if source == 0 else trc
    return ref[pl.ds(index * 2 * levels + x, levels, stride=2), :]


def pack_quad(dyn, trc, weight, m, quad, x, levels):
    rows = jnp.concatenate(
        [weight[x] * field_rows(dyn, trc, levels, which, x) for which in quad], 1
    )
    return select_dot2(rows, m)


def flat(ref):
    lead = 1
    for size in ref.shape[:-1]:
        lead *= size
    return ref.reshape(lead, LANES)


def runs_of(fields):
    runs = []
    for source, index in fields:
        if runs and runs[-1][0] == source and runs[-1][1] + runs[-1][2] == index:
            runs[-1][2] += 1
        else:
            runs.append([source, index, 1])
    return runs


def start_loads(quads, dyn_hbm, trc_hbm, buffer, sems):
    loads, b, count = [], 0, 0
    for quad in quads:
        copies = []
        for source, index, length in runs_of(quad):
            ref = dyn_hbm if source == 0 else trc_hbm
            copies.append(
                pltpu.make_async_copy(
                    ref.at[pl.ds(index, length)], buffer.at[pl.ds(b, length)], sems.at[count]
                )
            )
            b, count = b + length, count + 1
        for copy in copies:
            copy.start()
        loads.append(copies)
    return loads


def pack_kernel(levels, chunks, weights_too, dyn_hbm, trc_hbm, thick3, area_ref, m_ref, *rest):
    buffer, sems = rest[-2:]
    outs = rest[-2 - 2 * len(chunks) : -2]
    rest = rest[: -2 - 2 * len(chunks)]
    quads = [quad for chunk in chunks for quad in chunk]
    loads = start_loads(quads, dyn_hbm, trc_hbm, buffer, sems)
    fields, thick = flat(buffer), flat(thick3)
    weight = [area_ref[x : x + 1, :] * thick[pl.ds(x, levels, stride=2), :] for x in range(2)]
    m = m_ref[...]
    last = TYPES * len(chunks[0])
    if weights_too:
        mw_ref = rest[0]
        for x, out in ((0, outs[1]), (1, outs[0])):
            out[last, 0:levels, :] = select_dot3(weight[x], mw_ref[...])
            area = jnp.broadcast_to(area_ref[x : x + 1, :], (8, LANES))
            out[last, levels : levels + 1, :] = select_dot3(area, mw_ref[...])[0:1]
    if len(rest) == 4:
        own_ref, before_ref, after_ref = rest[:3]
        left = lane_iota(own_ref.shape[1]) < HALF
        for x, out in ((0, outs[1]), (1, outs[0])):
            out[last] = own_ref[x] + jnp.where(
                left, pltpu.roll(before_ref[x], HALF, 1), pltpu.roll(after_ref[x], HALF, 1)
            )
    number = 0
    for place, chunk in enumerate(chunks):
        for i in range(len(chunk)):
            for copy in loads[number]:
                copy.wait()
            where = [(1, NP * number + b) for b in range(NP)]
            for x, out in ((0, outs[2 * place + 1]), (1, outs[2 * place])):
                packed = pack_quad(None, fields, weight, m, where, x, levels)
                for kind in range(TYPES):
                    out[TYPES * i + kind, 0:levels, :] = packed[:, kind * LANES : (kind + 1) * LANES]
            number += 1


def ends_kernel(levels, ndyn, ntrc, dyn_hbm, trc_hbm, thick3, area_ref, after_ref, edge_ref, buffer, sems):
    groups = [[(0, i) for i in range(ndyn)]]
    groups += [[(1, i) for i in range(k, min(k + 11, ntrc))] for k in range(0, ntrc, 11)]
    loads = start_loads(groups, dyn_hbm, trc_hbm, buffer, sems)
    rows, thick = flat(buffer), flat(thick3)
    weight = [area_ref[x : x + 1, :] * thick[pl.ds(x, levels, stride=2), :] for x in range(2)]
    lane = lane_iota(levels)
    ends = jnp.where(lane < HALF, 0, LANES - 1)
    spot = lane % HALF
    count = ndyn + ntrc
    totals = [jnp.zeros((levels, LANES), F32)] * 2
    number = 0
    for group, copies in zip(groups, loads):
        for copy in copies:
            copy.wait()
        for _ in group:
            for x in range(2):
                here = pick_lanes(field_rows(None, rows, levels, (1, number), x), ends)
                totals[x] = jnp.where(spot == number, here, totals[x])
            number += 1
    for x in range(2):
        both = pick_lanes(weight[x], ends)
        edge_ref[x, 0:levels, :] = jnp.where(spot == count, 1.0, totals[x]) * both
        edge_ref[x, levels : levels + 1, :] = pick_lanes(
            jnp.broadcast_to(area_ref[x : x + 1, :], (8, LANES)), ends[0:8]
        )[0:1]


def remap_group(levels, windows, summed, rm, thick, al, ar, aq, rdt, tile_of, row_of, s_ref):
    rows = summed.shape[0]
    tiles = rows // 8
    q = summed * rm
    first = q[0:1]
    last = jnp.broadcast_to(q[levels - 1 : levels], (rows - levels + 2, LANES))
    s_ref[0, 8 : 8 + rows, :] = q
    s_ref[0, 7:8, :] = first
    s_ref[0, 8 + levels : 10 + rows, :] = last
    below = s_ref[0, 7 : 7 + rows, :]
    q = s_ref[0, 8 : 8 + rows, :]
    above = s_ref[0, 9 : 9 + rows, :]
    above_two = s_ref[0, 10 : 10 + rows, :]
    edge = 7.0 / 12.0 * (q + above) - 1.0 / 12.0 * (below + above_two)
    edge = jnp.clip(edge, jnp.minimum(q, above), jnp.maximum(q, above))
    s_ref[1, 8 : 8 + rows, :] = edge
    s_ref[1, 7:8, :] = first
    left = s_ref[1, 7 : 7 + rows, :]
    layer = thick * q
    through = prefix_rows(layer) - layer
    for j in range(tiles):
        low, high = windows[j][0] // 8, windows[j][1] // 8
        part = slice(8 * j, 8 * j + 8)
        tile, row = tile_of[part], row_of[part]
        got = None
        for v in range(low, high + 1):
            here = [
                jnp.take_along_axis(a[8 * v : 8 * v + 8], row, axis=0, mode="promise_in_bounds")
                for a in (through, left, edge, q)
            ]
            if got is None:
                got = here
            else:
                got = [jnp.where(tile == v, new, old) for new, old in zip(here, got)]
        s_ref[2, 8 + 8 * j : 16 + 8 * j, :] = (
            got[0] + al[part] * got[1] + ar[part] * got[2] + aq[part] * got[3]
        )
    s_ref[2, 7:8, :] = jnp.zeros((1, LANES), F32)
    return (s_ref[2, 8 : 8 + rows, :] - s_ref[2, 7 : 7 + rows, :]) * rdt


def column_surface(weights_surface, edge_surface):
    lane = lane_iota(8)
    spot, kind = lane // NP, lane % NP
    index = jnp.where(kind == 3, jnp.minimum(spot + 1, PART - 1), kind * PART + spot)
    inner = pick_lanes(weights_surface, index)
    return jnp.where((lane == 0) | (lane == LANES - 1), edge_surface, inner)


def setup_kernel(levels, nfields, own0, own1, from_up, from_down, row0, row1, edge_up, edge_down, p_ref, i_ref, e_ref, surface_ref, s_ref):
    windows = tile_windows(levels)
    rows = row0.shape[1]
    tiles = rows // 8
    row = row_iota(rows)
    lane = lane_iota(rows)
    inside = row < levels
    edge_lanes = jnp.where(lane < HALF, nfields, HALF + nfields)
    kept = []
    for base in range(4):
        x = base % 2
        own, got = ((own0, from_up), (own1, from_down))[x]
        eown, egot = ((row0, edge_up), (row1, edge_down))[x]
        if base < 2:
            mass = own[0] + got[0]
        else:
            summed = eown[0] + egot[0]
            mass = pick_lanes(summed, edge_lanes)
        area = mass[levels : levels + 1]
        mass = jnp.where(inside, mass, 1.0)
        thick = jnp.where(inside, mass / area, 1.0)
        after = top_pressure + prefix_rows(thick)
        surface = after[levels - 1 : levels]
        s_ref[0, 8 : 8 + rows, :] = after
        s_ref[0, 7:8, :] = jnp.full((1, LANES), top_pressure, F32)
        s_ref[1, 0:rows, :] = thick
        sigma = (row + 1).astype(F32) / levels
        sigma0 = row.astype(F32) / levels

        def target_at(s):
            return top_pressure * (1.0 - s) + s * s * surface + s * (1.0 - s) * mid_pressure

        target = target_at(sigma)
        rdt = jnp.where(inside, 1.0 / (target - target_at(sigma0)), 1.0)
        index, start, depth = [], [], []
        for j in range(tiles):
            low, high = windows[j]
            here = target[8 * j : 8 * j + 8]
            count = jnp.full((8, LANES), low, jnp.int32)
            source = jnp.broadcast_to(s_ref[0, 7 + low : 8 + low, :], (8, LANES))
            size = jnp.broadcast_to(s_ref[1, low : low + 1, :], (8, LANES))
            for k in range(low + 1, high + 1):
                edge_k = jnp.broadcast_to(s_ref[0, 7 + k : 8 + k, :], (8, LANES))
                size_k = jnp.broadcast_to(s_ref[1, k : k + 1, :], (8, LANES))
                reached = edge_k <= here
                count = jnp.where(reached, k, count)
                source = jnp.where(reached, edge_k, source)
                size = jnp.where(reached, size_k, size)
            index.append(count)
            start.append(source)
            depth.append(size)
        index, start, depth = (jnp.concatenate(a, 0) for a in (index, start, depth))
        f = jnp.clip((target - start) / depth, 0.0, 1.0)
        f2, f3 = f * f, f * f * f
        values = [
            1.0 / mass,
            thick,
            depth * (f - 2.0 * f2 + f3),
            depth * (f3 - f2),
            depth * (3.0 * f2 - 2.0 * f3),
            rdt,
        ]
        tile_of, row_of = index >> 3, index & 7
        if base < 2:
            for kind in range(TYPES):
                lanes = kind * PART + lane % PART
                group = 2 * kind + x
                for i, value in enumerate(values):
                    p_ref[group, i] = pick_lanes(value, lanes)
                i_ref[group, 0] = pick_lanes(tile_of, lanes)
                i_ref[group, 1] = pick_lanes(row_of, lanes)
            kept.append(jnp.broadcast_to(surface, (8, LANES)))
        else:
            e_ref[x] = remap_group(levels, windows, summed, *values, tile_of, row_of, s_ref)
            surface_ref[0:1, x * LANES : (x + 1) * LANES] = column_surface(
                kept[x], jnp.broadcast_to(surface, (8, LANES))
            )[0:1]


def remap_kernel(levels, ndyn, quads, aliased, extra, own0, own1, from_up, from_down, p_ref, i_ref, e_ref, mt_ref, *rest):
    if aliased:
        rest = rest[2 + extra :]
        dyn_ref, trc_ref = rest[:2]
        columns_ref = None
        rest = rest[2:]
    else:
        dyn_ref, trc_ref, columns_ref = rest[:3]
        rest = rest[3:]
    s_ref, packed_ref, out_ref, sems = rest
    windows = tile_windows(levels)
    rows = e_ref.shape[1]
    lane = lane_iota(levels)
    ends = (lane == 0) | (lane == LANES - 1)
    half = jnp.where(lane < HALF, 0, HALF)
    out_rows = flat(out_ref)
    fields = TYPES + 1

    def one_quad(i, edge_lane):
        for kind in range(TYPES):
            for x in range(2):
                group = 2 * kind + x
                own, got = ((own0, from_up), (own1, from_down))[x]
                summed = own[TYPES * i + kind] + got[TYPES * i + kind]
                values = [p_ref[group, n] for n in range(PARAMS)]
                packed_ref[x * rows : (x + 1) * rows, kind * LANES : (kind + 1) * LANES] = remap_group(
                    levels, windows, summed, *values, i_ref[group, 0], i_ref[group, 1], s_ref.at[x]
                )
        wide = select_dot2(packed_ref[...], mt_ref[...])
        for b in range(fields):
            for x in range(2):
                value = wide[x * rows : x * rows + levels, b * LANES : (b + 1) * LANES]
                outer = pick_lanes(e_ref[x, 0:levels, :], half + edge_lane(b))
                value = jnp.where(ends, outer, value)
                out_rows[pl.ds((i * fields + b) * 2 * levels + x, levels, stride=2), :] = value
                if columns_ref is not None and isinstance(i, int) and i == 0:
                    columns_ref[b, 0:levels, x * LANES : (x + 1) * LANES] = value

    table = [[index + (0 if source == 0 else ndyn) for source, index in quad] for quad in quads]
    start = len(quads) - 1 if aliased else max(len(quads) - 1, 1)
    while start > 1 and table[start] == [v + fields for v in table[start - 1]]:
        start -= 1
    for i in range(start):
        one_quad(i, lambda b: table[i][b])

    @pl.loop(start, len(quads))
    def _(i):
        one_quad(i, lambda b: table[start][b] + fields * (i - start))

    copies = []
    for i, quad in enumerate(quads):
        b = 0
        while b < fields:
            source, index = quad[b]
            length = 1
            while b + length < fields and quad[b + length] == (source, index + length):
                length += 1
            target = dyn_ref if source == 0 else trc_ref
            copies.append(
                pltpu.make_async_copy(
                    out_ref.at[pl.ds(i * fields + b, length)],
                    target.at[pl.ds(index, length)],
                    sems.at[len(copies)],
                )
            )
            b += length
    for copy in copies:
        copy.start()
    for copy in copies:
        copy.wait()


def turn(row):
    return jnp.transpose(jnp.broadcast_to(row, (LANES, LANES)))


def route_kernel(devices, owner_ref, counts_ref, position_ref):
    capacity = 2 * 2 * LANES // devices
    owner = owner_ref[...].astype(F32)
    rows = [owner[x : x + 1] for x in range(2)]
    down = [turn(r) for r in rows]
    r, c = row_iota(LANES), lane_iota(LANES)
    ranks = []
    for x in range(2):
        same = jnp.where((down[x] == rows[x]) & (r < c), 1.0, 0.0)
        rank = jnp.sum(same, axis=0, keepdims=True)
        if x == 1:
            rank = rank + jnp.sum(jnp.where(down[0] == rows[1], 1.0, 0.0), axis=0, keepdims=True)
        ranks.append(rank)
        position_ref[0:1, x * LANES : (x + 1) * LANES] = (rows[x] * capacity + rank).astype(jnp.int32)
    device = lax.broadcasted_iota(jnp.int32, (devices, LANES), 0).astype(F32)
    count = sum(
        jnp.sum(jnp.where(device == row, 1.0, 0.0), axis=1, keepdims=True) for row in rows
    )
    counts_ref[...] = jnp.broadcast_to(count[:, :, None], (devices, 1, LANES))


def slot_rows(devices, counts_ref, columns):
    capacity = 2 * columns // devices
    slots = devices * capacity
    counts = jnp.concatenate([counts_ref[d] for d in range(devices)], 0)
    r = lax.broadcasted_iota(jnp.int32, (slots, devices), 0) // capacity
    d = lax.broadcasted_iota(jnp.int32, (slots, devices), 1)
    before = dot(jnp.where(d < r, 1.0, 0.0).astype(BF16), counts.astype(BF16))
    own = dot(jnp.where(d == r, 1.0, 0.0).astype(BF16), counts.astype(BF16))
    rank = (lax.broadcasted_iota(jnp.int32, (slots, LANES), 0) % capacity).astype(F32)
    slot = jnp.where(rank < own, before + rank, -1.0).astype(jnp.int32)
    parts = [
        jnp.where(slot == lane_iota(slots) + LANES * g, 1.0, 0.0) for g in range(columns // LANES)
    ]
    return jnp.concatenate(parts, 1).astype(BF16)


def three_parts(x):
    top = x.astype(BF16)
    rest = x - top.astype(F32)
    mid = rest.astype(BF16)
    return top, mid, (rest - mid.astype(F32)).astype(BF16)


def dot_nt(a, b):
    return lax.dot_general(a, b, (((1,), (1,)), ((), ())), preferred_element_type=F32)


def dot_tn(a, b):
    return lax.dot_general(a, b, (((0,), (0,)), ((), ())), preferred_element_type=F32)


def to_slots(hot, values):
    return sum(dot_nt(hot, part) for part in three_parts(values))


def from_slots(hot, values):
    turned = jnp.transpose(values)
    return sum(dot(part, hot) for part in three_parts(turned))


def pad_rows(x):
    return jnp.concatenate([x, jnp.zeros((LANES - x.shape[0], x.shape[1]), x.dtype)], 0)


def cloud_kernel(devices, counts_ref, cloud_ref, *rest):
    send_ref = rest[-1]
    hot = slot_rows(devices, counts_ref, cloud_ref.shape[1])
    send_ref[...] = to_slots(hot, pad_rows(cloud_ref[...]))


def final_kernel(devices, levels, counts_ref, got_ref, cloud_ref):
    hot = slot_rows(devices, counts_ref, cloud_ref.shape[1])
    cloud_ref[...] = from_slots(hot, got_ref[...])[0:levels]


def physics_kernel(levels, columns_ref, got_ref, position_ref, surface_ref, warm_ref, inc_ref, send_ref, a_ref, g_ref):
    columns = position_ref.shape[1]
    slots = got_ref.shape[0]
    hot = jnp.where(
        position_ref[...] == lax.broadcasted_iota(jnp.int32, (slots, columns), 0), 1.0, 0.0
    ).astype(BF16)
    cloud = from_slots(hot, got_ref[...])[0:levels]
    t, v, c, r = (columns_ref[b, 0:levels, :] for b in range(4))
    surface = surface_ref[...]
    row = lax.broadcasted_iota(jnp.int32, (levels, columns), 0)

    def target_at(s):
        return top_pressure * (1.0 - s) + s * s * surface + s * (1.0 - s) * mid_pressure

    upper = target_at(row.astype(F32) / levels)
    lower = target_at((row + 1).astype(F32) / levels)
    layer = lower - upper
    middle = 0.5 * (lower + upper)
    celsius = 10.0 * t
    saturation = 3.8 / middle * jnp.exp(17.27 * celsius / (celsius + 237.3))
    condensed = jnp.maximum((v - saturation) / (1.0 + kappa_sat * saturation), -c)
    v1 = v - condensed
    c1 = c + condensed
    t1 = t + phase_change_warming * condensed
    converted = c1 * (1.0 - jnp.exp(-(auto_rate * cloud + accrete_rate * r)))
    warm_rows = warm_ref[...]
    warm = jnp.concatenate([warm_rows[0:1], warm_rows[1:2]], 1) == 1
    c2 = jnp.where(warm, c1 - converted, c1)
    r1 = jnp.where(warm, r + converted, r)
    fall = fall_rate * (0.5 + cloud)
    share = 1.0 / (1.0 + fall)
    a_ref[0:levels, :] = r1 * layer
    g_ref[0:levels, :] = fall * share
    held = jnp.zeros((1, columns), F32)
    for k in range(levels):
        held = a_ref[k : k + 1, :] + held
        a_ref[k : k + 1, :] = held
        held = g_ref[k : k + 1, :] * held
    r2 = jnp.where(warm, a_ref[0:levels, :] * share / layer, r1)
    out = flat(inc_ref)
    for b, change in enumerate((t1 - t, v1 - v, c2 - c, r2 - r)):
        for x in range(2):
            out[pl.ds(b * 2 * levels + x, levels, stride=2), :] = change[:, x * LANES : (x + 1) * LANES]
    goal = jnp.clip((v1 / saturation - 0.7) / 0.3, 0.05, 1.0)
    send_ref[...] = to_slots(hot, pad_rows(cloud + 0.5 * (goal - cloud)))


def ring(axis):
    size = lax.axis_size(axis)
    up = [(i, (i + 1) % size) for i in range(size)]
    return up, [(j, i) for i, j in up]


def shape(*dims, dtype=F32):
    return jax.ShapeDtypeStruct(dims, dtype)


def local(dynamics, tracers, thickness, area_weight, cloud_frac, owner, warm_mask):
    levels = thickness.shape[0]
    ndyn, ntrc = dynamics.shape[0], tracers.shape[0]
    nfields = ndyn + ntrc
    rows = -(-(levels + 1) // 8) * 8
    columns = 2 * LANES
    devices = lax.axis_size(("gx", "gy"))
    slots = devices * (2 * columns // devices)
    axes = ("gx", "gy")
    fields = [(0, i) for i in range(1, ndyn)] + [(1, i) for i in range(3, ntrc)]
    quads = [fields[i : i + 4] for i in range(0, len(fields), 4)]
    first_quad = [(0, 0), (1, 0), (1, 1), (1, 2)]
    quads = [first_quad] + quads
    chunks, begin = [], 0
    for length in CHUNKS:
        chunks.append(quads[begin : begin + length])
        begin += length
    assert begin == len(quads)
    matrix = pack_matrix()
    m = jnp.asarray(matrix, BF16)
    mt = jnp.asarray(matrix.T, BF16)
    mw = jnp.asarray(weight_matrix(), BF16)
    up, down = ring("gx")
    right, left = ring("gy")
    fields_in = (dynamics, tracers, thickness, area_weight)

    packed, received = [None] * len(chunks), [None] * len(chunks)

    def send(numbers, extra, args, specs, name):
        parts = [chunks[n] for n in numbers]
        total = sum(len(part) for part in parts)
        sent = pl.pallas_call(
            lambda *refs: pack_kernel(levels, parts, numbers[0] == 0, *refs),
            out_shape=tuple(
                shape(TYPES * len(part) + extra, rows, LANES) for part in parts for _ in range(2)
            ),
            in_specs=[ANY, ANY] + [VM] * 3 + specs,
            out_specs=(VM,) * (2 * len(parts)),
            scratch_shapes=[
                pltpu.VMEM((NP * total, levels, 2, LANES), F32),
                pltpu.SemaphoreType.DMA((2 * total,)),
            ],
            compiler_params=params(BIG),
            cost_estimate=cost(EARLY),
            name=name,
        )(*fields_in, m, *args)
        for i, n in enumerate(numbers):
            packed[n] = (sent[2 * i], sent[2 * i + 1])
            received[n] = (
                lax.ppermute(sent[2 * i], "gx", up),
                lax.ppermute(sent[2 * i + 1], "gx", down),
            )

    counts, position = pl.pallas_call(
        lambda *refs: route_kernel(devices, *refs),
        out_shape=(shape(devices, 1, LANES), shape(1, columns, dtype=jnp.int32)),
        in_specs=[VM],
        out_specs=(VM, VM),
        compiler_params=params(BIG),
        cost_estimate=cost(EARLY),
        name="route",
    )(owner)
    counts_in = lax.all_to_all(counts, axes, split_axis=0, concat_axis=0, tiled=True)

    send([0], 1, (mw,), [VM], "first_pack")

    edges = pl.pallas_call(
        lambda *refs: ends_kernel(levels, ndyn, ntrc, *refs),
        out_shape=shape(2, rows, LANES),
        in_specs=[ANY, ANY, VM, VM, ANY],
        out_specs=VM,
        scratch_shapes=[
            pltpu.VMEM((nfields, levels, 2, LANES), F32),
            pltpu.SemaphoreType.DMA((8,)),
        ],
        compiler_params=params(BIG),
        cost_estimate=cost(EARLY),
        name="ends",
    )(*fields_in, packed[0][0])
    before = lax.ppermute(edges, "gy", right)
    after = lax.ppermute(edges, "gy", left)

    cloud_out = pl.pallas_call(
        lambda *refs: cloud_kernel(devices, *refs),
        out_shape=shape(slots, LANES),
        in_specs=[VM] * 2 + [ANY] * 3,
        out_specs=VM,
        compiler_params=params(),
        cost_estimate=cost(2),
        name="cloud_send",
    )(counts_in, cloud_frac, packed[0][0], *received[0])
    cloud_in = lax.all_to_all(cloud_out, axes, split_axis=0, concat_axis=0, tiled=True)

    send([1], 1, (edges, before, after, cloud_out), [VM] * 3 + [ANY], "second_pack")

    send(list(range(2, len(chunks))), 0, (packed[1][0],), [ANY], "pack")
    def one_group(number):
        group = TYPES * len(chunks[number])
        return pl.BlockSpec((1, rows, LANES), lambda i: (group, 0, 0))

    def full(*dims):
        return pl.BlockSpec(dims, lambda i: (0,) * len(dims))

    weights, indices, edge_values, surface = pl.pallas_call(
        lambda *refs: setup_kernel(levels, nfields, *refs),
        grid=(1,),
        out_shape=(
            shape(2 * TYPES, PARAMS, rows, LANES),
            shape(2 * TYPES, 2, rows, LANES, dtype=jnp.int32),
            shape(2, rows, LANES),
            shape(1, columns),
        ),
        in_specs=[one_group(0)] * 4 + [one_group(1)] * 4,
        out_specs=(
            full(2 * TYPES, PARAMS, rows, LANES),
            full(2 * TYPES, 2, rows, LANES),
            full(2, rows, LANES),
            full(1, columns),
        ),
        scratch_shapes=[pltpu.VMEM((3, rows + 16, LANES), F32)],
        compiler_params=params(BIG),
        cost_estimate=cost(5),
        name="column_setup",
    )(packed[0][1], packed[0][0], *received[0], packed[1][1], packed[1][0], *received[1])

    def remap(chunk, own0, own1, got_up, got_down, so_far, follows=()):
        aliased = so_far is not None
        out_shape = (shape(*dynamics.shape), shape(*tracers.shape))
        args = [own0, own1, got_up, got_down, weights, indices, edge_values, mt]
        in_specs = [VM] * 8
        out_specs = (ANY, ANY)
        aliases = {}
        if aliased:
            args += list(so_far) + list(follows)
            in_specs += [ANY] * (2 + len(follows))
            aliases = {8: 0, 9: 1}
        else:
            out_shape += (shape(4, rows, columns),)
            out_specs += (VM,)
        return pl.pallas_call(
            lambda *refs: remap_kernel(levels, ndyn, chunk, aliased, len(follows), *refs),
            out_shape=out_shape,
            in_specs=in_specs,
            out_specs=out_specs,
            input_output_aliases=aliases,
            scratch_shapes=[
                pltpu.VMEM((2, 3, rows + 16, LANES), F32),
                pltpu.VMEM((2 * rows, TYPES * LANES), F32),
                pltpu.VMEM((4 * len(chunk), levels, 2, LANES), F32),
                pltpu.SemaphoreType.DMA((2 * len(chunk),)),
            ],
            compiler_params=params(),
            cost_estimate=cost(2 * len(chunk)),
            name="remap",
        )(*args)

    dyn_new, trc_new, physics_columns = remap(
        chunks[0], packed[0][1], packed[0][0], *received[0], None
    )

    increments, next_out = pl.pallas_call(
        lambda *refs: physics_kernel(levels, *refs),
        out_shape=(shape(4, levels, 2, LANES), shape(slots, LANES)),
        in_specs=[VM] * 5,
        out_specs=(VM,) * 2,
        scratch_shapes=[pltpu.VMEM((rows, columns), F32)] * 2,
        compiler_params=params(),
        cost_estimate=cost(5),
        name="physics",
    )(physics_columns, cloud_in, position, surface, warm_mask)
    next_in = lax.all_to_all(next_out, axes, split_axis=0, concat_axis=0, tiled=True)

    done = (dyn_new, trc_new)
    for number, chunk in list(enumerate(chunks))[1:]:
        done = remap(chunk, packed[number][1], packed[number][0], *received[number], done, (next_out,) if number > 1 else ())

    cloud_next = pl.pallas_call(
        lambda *refs: final_kernel(devices, levels, *refs),
        out_shape=shape(levels, columns),
        in_specs=[VM] * 2,
        out_specs=VM,
        compiler_params=params(),
        cost_estimate=cost(2),
        name="cloud_receive",
    )(counts_in, next_in)
    return (done[0], done[1], increments, cloud_next)


def solution(mesh):
    placed = (
        P(None, None, "gx", "gy"),
        P(None, None, "gx", "gy"),
        P(None, "gx", "gy"),
        P("gx", "gy"),
        P(None, ("gx", "gy")),
        P("gx", "gy"),
        P("gx", "gy"),
    )
    return jax.shard_map(
        local,
        mesh=mesh,
        in_specs=placed,
        out_specs=(
            P(None, None, "gx", "gy"),
            P(None, None, "gx", "gy"),
            P(None, None, "gx", "gy"),
            P(None, ("gx", "gy")),
        ),
        check_vma=False,
    )
```
